32 devices in a mesh: face: 4 (over z), tile: 8 (over y, x, core).
Axes of the slice: x: 2, y: 2, z: 4, core: 2. Of those that a mesh axis runs over, the one named last changes fastest.
Arguments:
- fields: bfloat16 [768, 384, 128], P('tile', 'face'), may hold values from -6 to 6
- first_kernel_taps: bfloat16 [9, 128, 128], replicated, may hold values from -0.1875 to 0.1875
- first_conv_bias: float32 [128], replicated, may hold values from -0.5 to 0.5
- second_kernel_taps: bfloat16 [9, 128, 128], replicated, may hold values from -0.1875 to 0.1875
- second_conv_bias: float32 [128], replicated, may hold values from -0.5 to 0.5
- obs_weight: bfloat16 [128, 128], replicated, may hold values from -0.5 to 0.5
- obs_values: bfloat16 [32768, 128], P(('face', 'tile')), may hold values from -6 to 6
- obs_owner: int32 [32768, 1], P(('face', 'tile')), may hold values from 0 to 31; in each aligned block of 1024 rows (0 to 1023, 1024 to 2047, ...) at most 64 rows name the same one
- obs_cells: int32 [32768], P(('face', 'tile')), may hold values from 0 to 9215
- polar_neighbor_sector: int32 [4, 2], replicated, may hold values from 0 to 3, as said below
- polar_link_reversal: int32 [4, 2], replicated, may hold values from 0 to 1
Outputs:
- level_out: bfloat16 [768, 384, 128], P('tile', 'face')
The draws below stay inside these ranges and needn't reach their ends.
Inputs may be any that keep to these rules, and one draw needn't show every extreme that they name: `obs_owner`: among the rows of one device at most 64 name the same tile, and in every draw some device sends exactly 64 rows to one tile. `polar_neighbor_sector`: each column links the sectors in one cycle through all 4 of them; no sector names itself.
All inputs are finite; a program needn't handle non-finite values.
Results may differ from the reference program's by a relative error of at most 0.0034.
Values may be sent and summed in bfloat16 or wider, within the bound.
A program may use at most 64 MiB of HBM per device.

```python
import math
import jax
import jax.numpy as jnp
import numpy as np
from jax import lax

C = 128
F = 128
SIDE = 96
OBS_DEV = 1024
FIRST_DILATION = 2
SECOND_DILATION = 4
NFACES = 4
NTILES = 8
TILES = 32
LAT = 768
LON = 384
OBS = 32768
CAP = 64


def draw_polar_neighbor_sector(key, part):
    column_keys = jax.random.split(jax.random.fold_in(key, 7), 2)
    columns = []
    for column in range(2):
        order = jax.random.permutation(column_keys[column], NFACES).astype(jnp.int32)
        following = jnp.roll(order, -1)
        links = jnp.zeros((NFACES,), jnp.int32).at[order].set(following)
        columns.append(links)
    return jnp.stack(columns, axis=1).astype(jnp.int32)


def with_ends(values, own_key, low, largest):
    extent = values.shape
    spot = [jax.random.randint(jax.random.fold_in(own_key, axis), (), 0, extent[axis]) for axis in range(len(extent))]
    values = values.at[tuple(spot)].set(low)
    longest = extent.index(max(extent))
    spot[longest] = (spot[longest] + 1) % extent[longest]
    return values.at[tuple(spot)].set(largest)


def block_scale(stream_key, shape, shards, least, largest):
    factor_of = 1.0
    for axis_at, shards_of in shards:
        heights = jax.random.uniform(jax.random.fold_in(jax.random.fold_in(stream_key, 6), axis_at), (shards_of,), jnp.float32, least / len(shards), largest / len(shards))
        factor_of = factor_of * jnp.repeat(jnp.exp(heights), shape[axis_at] // shards_of).reshape((-1,) + (1,) * (len(shape) - 1 - axis_at))
    return factor_of


def assign_block(own_key, own, number, rows, count, top, limit, skew):
    ranking = jax.random.permutation(own_key, count)
    packed, usual = shares(count, rows * top, limit, skew, True), shares(count, rows * top, limit, skew, False)
    places = jnp.arange(count)

    def named(tallies, offset_by):
        used = int((tallies > 0).sum())
        fixed = max(1, used // 4)
        moved = fixed + (places - fixed + offset_by * (used - fixed)) % max(1, count - fixed)
        return jnp.zeros((count,), jnp.int32).at[ranking[jnp.where(places < fixed, places, moved)]].set(jnp.asarray(tallies, jnp.int32))

    tallies = jnp.where(number % 4 == 0, named(packed, number // 4), named(usual, number - number // 4 - 1))
    mixed = jax.random.permutation(jax.random.fold_in(own, 3), count)
    giver, taker = mixed[0:count // 2 * 2:2], mixed[1:count // 2 * 2:2]
    margin = jnp.minimum(tallies[giver] - 1, limit - tallies[taker]) // 2
    margin = jnp.where((giver == ranking[0]) | (taker == ranking[0]) | (tallies[taker] == 0), 0, jnp.maximum(margin, 0))
    moved = jax.random.randint(jax.random.fold_in(own, 4), (count // 2,), 0, 1 << 20) % (margin + 1)
    tallies = tallies.at[giver].add(-moved).at[taker].add(moved)
    items = jnp.searchsorted(jnp.cumsum(tallies), jnp.arange(rows * top), side="right").astype(jnp.int32)
    table = items.reshape(top, rows).T
    table = table[jax.random.permutation(jax.random.fold_in(own, 1), rows)]
    offset_by = jax.random.randint(jax.random.fold_in(own, 2), (rows, 1), 0, top)
    return jnp.take_along_axis(table, (jnp.arange(top)[None, :] + offset_by) % top, axis=1)


def shares(amount, total, bound, slope, full):
    loads = [(1 << 20) // math.isqrt(standing ** slope) + 1 for standing in range(1, amount + 1)]
    largest = bound if full else min(bound, max(-(-total // amount), total * loads[0] // sum(loads)))
    least = 1 if total - largest >= amount - 1 else 0
    counts, rest = [largest] + [least] * (amount - 1), total - largest - least * (amount - 1)
    while rest > 0:
        movable = [i for i in range(1, amount) if counts[i] < largest] or [i for i in range(1, amount) if counts[i] < bound]
        pool, budget = sum([loads[i] for i in movable]), rest
        for i in movable:
            addition = min(bound - counts[i], max(1, budget * loads[i] // pool), rest)
            counts[i] = counts[i] + addition
            rest = rest - addition
    return np.array(counts)


def normal_values(key, shape, spread, bound, shards=(), dtype=jnp.bfloat16):
    values = spread * jax.random.normal(key, shape, jnp.float32)
    if shards:
        values = values * block_scale(key, shape, shards, -0.22, 0.18)
    return jnp.clip(values, -bound, bound).astype(dtype)


def setup_inputs(seed: int = 0) -> dict:
    streams_of = jax.random.split(jax.random.key(seed), 12)
    fields = normal_values(streams_of[0], (LAT, LON, C), 1.0, 6.0, ((0, 8), (1, 4)))
    first_kernel_taps = normal_values(streams_of[1], (9, C, C), (9 * C) ** -0.5, 0.1875)
    first_conv_bias = jnp.clip(jax.random.uniform(streams_of[2], (C,), jnp.float32, -0.5, 0.5), -0.5, 0.5)
    second_kernel_taps = normal_values(streams_of[3], (9, C, C), (9 * C) ** -0.5, 0.1875)
    second_conv_bias = jnp.clip(jax.random.uniform(streams_of[4], (C,), jnp.float32, -0.5, 0.5), -0.5, 0.5)
    obs_weight = normal_values(streams_of[5], (F, C), F ** -0.5, 0.5)
    obs_values = normal_values(streams_of[6], (OBS, F), 1.0, 6.0, ((0, 32),))
    obs_owner_keys = jax.random.split(jax.random.fold_in(streams_of[7], 1), OBS // OBS_DEV)
    obs_owner_turns = jax.random.permutation(jax.random.fold_in(streams_of[7], 3), OBS // OBS_DEV)
    obs_owner = jax.vmap(lambda own, number: assign_block(jax.random.fold_in(streams_of[7], 2), own, number, OBS_DEV, TILES, 1, CAP, 2))(obs_owner_keys, obs_owner_turns).reshape((OBS, 1))
    obs_cells = with_ends(jax.random.randint(streams_of[8], (OBS,), 0, SIDE * SIDE), jax.random.fold_in(streams_of[8], 1), 0, (SIDE * SIDE) - 1).astype(jnp.int32)
    polar_neighbor_sector = draw_polar_neighbor_sector(jax.random.fold_in(streams_of[11], 71), 0)
    polar_link_reversal = with_ends(jax.random.randint(streams_of[10], (NFACES, 2), 0, 2), jax.random.fold_in(streams_of[10], 1), 0, 1).astype(jnp.int32)
    return dict(fields=fields, first_kernel_taps=first_kernel_taps, first_conv_bias=first_conv_bias, second_kernel_taps=second_kernel_taps, second_conv_bias=second_conv_bias, obs_weight=obs_weight, obs_values=obs_values, obs_owner=obs_owner, obs_cells=obs_cells, polar_neighbor_sector=polar_neighbor_sector, polar_link_reversal=polar_link_reversal)


def apply_stencil_taps(padded, kernel, bias_row, dilation, rows, cols):
    channels = padded.shape[-1]
    total = jnp.zeros((rows * cols, kernel.shape[-1]), jnp.float32)
    for tap_row in range(3):
        for tap_col in range(3):
            window = padded[tap_row * dilation: tap_row * dilation + rows, tap_col * dilation: tap_col * dilation + cols]
            total = total + jnp.dot(window.reshape(rows * cols, channels), kernel[tap_row * 3 + tap_col], preferred_element_type=jnp.float32)
    return total + bias_row.astype(jnp.float32)[None, :]


def spherical_convolve(grid, kernel, bias_row, dilation, polar_neighbor_sector, polar_link_reversal):
    lat_rows = grid.shape[0]
    lon_cols = grid.shape[1]
    sector_side_length = lon_cols // NFACES
    loop = jnp.concatenate([grid[:, lon_cols - dilation:], grid, grid[:, :dilation]], axis=1)
    outputs = []
    for sector in range(NFACES):
        strip = loop[:, sector * sector_side_length: sector * sector_side_length + sector_side_length + 2 * dilation]
        north_start = (polar_neighbor_sector[sector, 0] * sector_side_length).astype(jnp.int32)
        south_start = (polar_neighbor_sector[sector, 1] * sector_side_length).astype(jnp.int32)
        north = lax.dynamic_slice_in_dim(loop[:dilation], north_start, sector_side_length + 2 * dilation, 1)[::-1]
        north = jnp.where(polar_link_reversal[sector, 0] == 1, north[:, ::-1], north)
        south = lax.dynamic_slice_in_dim(loop[lat_rows - dilation:], south_start, sector_side_length + 2 * dilation, 1)[::-1]
        south = jnp.where(polar_link_reversal[sector, 1] == 1, south[:, ::-1], south)
        padded = jnp.concatenate([north, strip, south], axis=0)
        result = apply_stencil_taps(padded, kernel, bias_row, dilation, lat_rows, sector_side_length)
        outputs.append(result.reshape(lat_rows, sector_side_length, -1))
    return jnp.concatenate(outputs, axis=1)


def reference(fields, first_kernel_taps, first_conv_bias, second_kernel_taps, second_conv_bias, obs_weight, obs_values, obs_owner, obs_cells, polar_neighbor_sector, polar_link_reversal):
    lat_rows = fields.shape[0]
    lon_cols = fields.shape[1]
    sector_side_length = lon_cols // NFACES
    first_activation = jax.nn.gelu(spherical_convolve(fields, first_kernel_taps, first_conv_bias, FIRST_DILATION, polar_neighbor_sector, polar_link_reversal), approximate=True)
    encoded = jnp.dot(obs_values, obs_weight, preferred_element_type=jnp.float32)
    owner = obs_owner[:, 0]
    lat_index = (owner % NTILES) * sector_side_length + obs_cells // sector_side_length
    lon_index = (owner // NTILES) * sector_side_length + obs_cells % sector_side_length
    inject = jnp.zeros((lat_rows, lon_cols, encoded.shape[1]), jnp.float32).at[lat_index, lon_index].add(encoded)
    blended_features = (first_activation + inject).astype(jnp.bfloat16)
    second_activation = spherical_convolve(blended_features, second_kernel_taps, second_conv_bias, SECOND_DILATION, polar_neighbor_sector, polar_link_reversal)
    return (fields.astype(jnp.float32) + jax.nn.gelu(second_activation, approximate=True)).astype(jnp.bfloat16)
```

```python
import functools

import jax
import jax.numpy as jnp
from jax import lax
from jax.experimental import pallas as pl
from jax.experimental.pallas import tpu as pltpu
from jax.sharding import PartitionSpec as P

FIRST_DILATION = 2
SECOND_DILATION = 4
MESH = pl.DeviceIdType.MESH
LANES = 128
EDGE = 16
VMEM_LIMIT = 56 * 1024 * 1024


def pack_columns(tile, d, east):
    rows, _, ch = tile.shape
    per = 8 // d
    half = tile[:, 8:] if east else tile[:, :8]
    grouped = half.reshape(rows // per, per, 8, ch)
    sub = lax.broadcasted_iota(jnp.int32, (rows // per, 8, ch), 1)
    out = None
    for j in range(per):
        shift = (j * d - (8 - d if east else 0)) % 8
        part = grouped[:, j]
        if shift:
            part = pltpu.roll(part, shift, 1)
        out = part if out is None else jnp.where(sub >= j * d, part, out)
    return out.reshape(rows // (2 * per), EDGE, ch).astype(jnp.bfloat16)


def unpack_columns(packed, d, west):
    count, _, ch = packed.shape
    per = 8 // d
    pieces = packed.astype(jnp.float32).reshape(2 * count, 8, ch)
    parts = []
    for j in range(per):
        shift = ((8 - d if west else 0) - j * d) % 8
        parts.append(pltpu.roll(pieces, shift, 1) if shift else pieces)
    return jnp.stack(parts, axis=1).reshape(2 * count * per, 8, ch)


def join_edge(east_tile, west_tile):
    east = east_tile.astype(jnp.float32)
    west = west_tile.astype(jnp.float32)
    axis = east.ndim - 2
    return jnp.concatenate(
        [lax.slice_in_dim(east, 0, 8, axis=axis), lax.slice_in_dim(west, 8, 16, axis=axis)], axis=axis
    ).astype(jnp.bfloat16)


def pack_kernel(
    dest_count, slots, cell_total, d,
    owner_ref, cells_ref, values_ref, west_ref, east_ref,
    rows_out, cells_out, pw_out, pe_out,
):
    obs = owner_ref.shape[1]
    owner = owner_ref[...]
    dests = lax.broadcasted_iota(jnp.int32, (dest_count, obs), 0)
    onehot = jnp.where(dests == owner, 1.0, 0.0)
    before = (
        lax.broadcasted_iota(jnp.int32, (obs, obs), 0) < lax.broadcasted_iota(jnp.int32, (obs, obs), 1)
    )
    ranks = jnp.dot(
        onehot.astype(jnp.bfloat16),
        jnp.where(before, 1.0, 0.0).astype(jnp.bfloat16),
        preferred_element_type=jnp.float32,
    )
    rank = jnp.sum(ranks * onehot, axis=0, keepdims=True).astype(jnp.int32)
    target = owner * slots + rank
    cells = cells_ref[...]
    kind = lax.broadcasted_iota(jnp.int32, (8, obs), 0)
    codes = jnp.where(kind == 0, cells // LANES, jnp.where(kind == 1, cells % LANES, 1))
    codes = codes.astype(jnp.float32).astype(jnp.bfloat16)
    cells_out[...] = jnp.full(cells_out.shape, cell_total, jnp.int32)
    values = values_ref[...]
    block = min(512, dest_count * slots)
    for base in range(0, dest_count * slots, block):
        wanted = base + lax.broadcasted_iota(jnp.int32, (block, obs), 0)
        match = jnp.where(wanted == target, 1.0, 0.0).astype(jnp.bfloat16)
        rows = jnp.dot(match, values, preferred_element_type=jnp.float32).astype(jnp.bfloat16)
        first = base // slots
        rows_out[first : first + block // slots] = rows.reshape(block // slots, slots, rows.shape[-1])
        got = lax.dot_general(
            codes, match, (((1,), (1,)), ((), ())), preferred_element_type=jnp.float32
        )
        found = (got[0:1] * LANES + got[1:2]).astype(jnp.int32)
        found = jnp.where(got[2:3] > 0.5, found, cell_total)
        for j in range(block // slots):
            cells_out[first + j, :, :slots] = found[:, j * slots : (j + 1) * slots]
    pw_out[...] = pack_columns(west_ref[...].astype(jnp.float32), d, False)
    pe_out[...] = pack_columns(east_ref[...].astype(jnp.float32), d, True)


def halo_sends(faces, tiles, d, grid, pw, pe, hw, he, north, south, corners, polar):
    s, t = lax.axis_index("face"), lax.axis_index("tile")
    rows, cols = grid.shape[0], grid.shape[1]
    east, west = lax.rem(s + 1, faces), lax.rem(s + faces - 1, faces)
    last, first = pl.ds(rows - d, d), pl.ds(0, d)
    right, left = pl.ds(cols - EDGE, EDGE), pl.ds(0, EDGE)
    not_top, not_low = t > 0, t < tiles - 1
    up, down = t - 1, t + 1
    plan = [
        (None, None, pe, hw, (east, t)),
        (None, None, pw, he, (west, t)),
        (not_low, not_top, grid.at[last], north, (s, down)),
        (not_top, not_low, grid.at[first], south, (s, up)),
        (not_low, not_top, grid.at[last, right], corners.at[0], (east, down)),
        (not_low, not_top, grid.at[last, left], corners.at[1], (west, down)),
        (not_top, not_low, grid.at[first, right], corners.at[2], (east, up)),
        (not_top, not_low, grid.at[first, left], corners.at[3], (west, up)),
    ]
    for k in range(1, faces):
        to = (lax.rem(s + k, faces), t)
        plan.append((t == 0, t == 0, grid.at[first], polar.at[s], to))
    for k in range(1, faces):
        to = (lax.rem(s + k, faces), t)
        plan.append((t == tiles - 1, t == tiles - 1, grid.at[last], polar.at[s], to))
    return plan


def guarded(cond, action):
    if cond is None:
        action()
    else:
        pl.when(cond)(action)


def start_halo(plan, send_sem, recv_sem):
    copies = []
    for i, (sends, receives, src, dst, to) in enumerate(plan):
        copy = pltpu.make_async_remote_copy(
            src_ref=src, dst_ref=dst, send_sem=send_sem.at[i], recv_sem=recv_sem.at[i],
            device_id=to, device_id_type=MESH,
        )
        guarded(sends, copy.start)
        copies.append((sends, receives, copy))
    return copies


def wait_halo(copies):
    for sends, receives, copy in copies:
        guarded(sends, copy.wait_send)
        guarded(receives, copy.wait_recv)


def own_polar(grid, polar, d, tiles, sem):
    s, t = lax.axis_index("face"), lax.axis_index("tile")
    top = pltpu.make_async_copy(grid.at[pl.ds(0, d)], polar.at[s], sem)
    low = pltpu.make_async_copy(grid.at[pl.ds(grid.shape[0] - d, d)], polar.at[s], sem)
    return [(t == 0, top), (t == tiles - 1, low)]


def first_exchange_kernel(
    faces, tiles, d, grid, pw, pe, rows, cells,
    hw, he, north, south, corners, polar, rows_in, cells_in,
    send_sem, recv_sem, row_send, row_recv, cell_send, cell_recv, own_sem,
):
    count = faces * tiles
    me = lax.axis_index("face") * tiles + lax.axis_index("tile")
    barrier = pltpu.get_barrier_semaphore()

    def device(k):
        other = lax.rem(me + k, count)
        return other, (other // tiles, lax.rem(other, tiles))

    def greet(k, carry):
        _, to = device(k)
        pl.semaphore_signal(barrier, inc=1, device_id=to, device_id_type=MESH)
        return carry

    lax.fori_loop(1, count, greet, 0)
    own_rows = pltpu.make_async_copy(rows.at[me], rows_in.at[me], own_sem.at[0])
    own_cells = pltpu.make_async_copy(cells.at[me], cells_in.at[me], own_sem.at[1])
    own_rows.start()
    own_cells.start()
    own = own_polar(grid, polar, d, tiles, own_sem.at[2])
    for cond, copy in own:
        guarded(cond, copy.start)
    pl.semaphore_wait(barrier, count - 1)
    copies = start_halo(
        halo_sends(faces, tiles, d, grid, pw, pe, hw, he, north, south, corners, polar), send_sem, recv_sem
    )

    def row_copy(k):
        other, to = device(k)
        return pltpu.make_async_remote_copy(
            src_ref=rows.at[other], dst_ref=rows_in.at[me],
            send_sem=row_send.at[k], recv_sem=row_recv.at[k], device_id=to, device_id_type=MESH,
        )

    def cell_copy(k):
        other, to = device(k)
        return pltpu.make_async_remote_copy(
            src_ref=cells.at[other], dst_ref=cells_in.at[me],
            send_sem=cell_send.at[k], recv_sem=cell_recv.at[k], device_id=to, device_id_type=MESH,
        )

    def send(k, carry):
        row_copy(k).start()
        cell_copy(k).start()
        return carry

    def finish(k, carry):
        row_copy(k).wait()
        cell_copy(k).wait()
        return carry

    lax.fori_loop(1, count, send, 0)
    wait_halo(copies)
    for cond, copy in own:
        guarded(cond, copy.wait)
    own_rows.wait()
    own_cells.wait()
    lax.fori_loop(1, count, finish, 0)


def second_exchange_kernel(
    faces, tiles, d, grid, pw, pe, hw, he, north, south, corners, polar, send_sem, recv_sem, own_sem
):
    s, t = lax.axis_index("face"), lax.axis_index("tile")
    barrier = pltpu.get_barrier_semaphore()

    def greet(to):
        pl.semaphore_signal(barrier, inc=1, device_id=to, device_id_type=MESH)

    east, west = lax.rem(s + 1, faces), lax.rem(s + faces - 1, faces)
    greet((east, t))
    greet((west, t))

    @pl.when(t > 0)
    def _():
        for f in (east, s, west):
            greet((f, t - 1))

    @pl.when(t < tiles - 1)
    def _():
        for f in (east, s, west):
            greet((f, t + 1))

    polar_end = (t == 0) | (t == tiles - 1)

    @pl.when(polar_end)
    def _():
        for k in range(2, faces - 1):
            greet((lax.rem(s + k, faces), t))

    own = own_polar(grid, polar, d, tiles, own_sem.at[0])
    for cond, copy in own:
        guarded(cond, copy.start)

    @pl.when(polar_end)
    def _():
        pl.semaphore_wait(barrier, 5 + faces - 3)

    @pl.when(jnp.logical_not(polar_end))
    def _():
        pl.semaphore_wait(barrier, 8)

    copies = start_halo(
        halo_sends(faces, tiles, d, grid, pw, pe, hw, he, north, south, corners, polar), send_sem, recv_sem
    )
    wait_halo(copies)
    for cond, copy in own:
        guarded(cond, copy.wait)


def fill_padded(faces, tiles, d, pad, grid, hw, he, north, south, corners, polar, link, turn):
    s, t = lax.axis_index("face"), lax.axis_index("tile")
    rows, cols = grid.shape[0], grid.shape[1]
    wide = cols + EDGE
    pad[d : d + rows, :cols] = grid[...]
    pad[d : d + rows, cols:] = jnp.concatenate(
        [unpack_columns(he[...], d, False), unpack_columns(hw[...], d, True)], axis=1
    ).astype(jnp.bfloat16)

    def from_pole(base, column):
        p = link[s, column]
        east, west = lax.rem(p + 1, faces), lax.rem(p + faces - 1, faces)
        here = lax.broadcasted_iota(jnp.int32, (wide, wide), 0)
        there = lax.broadcasted_iota(jnp.int32, (wide, wide), 1)
        mirrored = jnp.where(here < cols, cols - 1 - here, wide + cols - 1 - here)
        source = jnp.where(turn[s, column] == 1, mirrored, here)
        move = jnp.where(there == source, 1.0, 0.0).astype(jnp.bfloat16)
        for i in range(d):
            k = d - 1 - i
            edge = join_edge(polar[east, k, :EDGE], polar[west, k, cols - EDGE :])
            line = jnp.concatenate([polar[p, k], edge], axis=0)
            pad[base + i] = jnp.dot(move, line, preferred_element_type=jnp.float32).astype(jnp.bfloat16)

    @pl.when(t == 0)
    def _():
        from_pole(0, 0)

    @pl.when(t > 0)
    def _():
        pad[:d, :cols] = north[...]
        pad[:d, cols:] = join_edge(corners[1], corners[0])

    @pl.when(t == tiles - 1)
    def _():
        from_pole(d + rows, 1)

    @pl.when(t < tiles - 1)
    def _():
        pad[d + rows :, :cols] = south[...]
        pad[d + rows :, cols:] = join_edge(corners[3], corners[2])


def fill_taps(taps, wide_taps):
    channels, features = taps.shape[1], taps.shape[2]
    for a in range(3):
        for e in range(3):
            wide_taps[a * channels : (a + 1) * channels, e * features : (e + 1) * features] = taps[3 * a + e]


def conv_rows(pad, wide_taps, bias, d, start, count, cols):
    wide = cols + EDGE
    features = bias.shape[-1]
    lines = [
        pad[pl.ds(start + a * d, count)].reshape(count * wide, pad.shape[-1]) for a in range(3)
    ]
    product = jnp.dot(
        jnp.concatenate(lines, axis=1), wide_taps[...], preferred_element_type=jnp.float32
    ).reshape(count, wide, 3 * features)
    low = pltpu.roll(product[:, :, :features], d, 1)
    high = pltpu.roll(product[:, :, 2 * features :], wide - d, 1)
    total = low + product[:, :, features : 2 * features] + high
    return total[:, :cols] + bias[...].reshape(1, 1, features)


def first_compute_kernel(
    faces, tiles, d, d_next, step_rows,
    link, turn, cells, grid, hw, he, north, south, corners, polar, taps, bias, values, weight,
    mixed, pw_out, pe_out, pad, wide_taps, inject, encoded,
):
    rows, cols = grid.shape[0], grid.shape[1]
    sources, slots, features = values.shape
    channels = bias.shape[-1]
    cell_total = rows * cols
    fill_taps(taps, wide_taps)
    encoded[...] = jnp.dot(
        values[...].reshape(sources * slots, features), weight[...], preferred_element_type=jnp.float32
    )
    inject[...] = jnp.zeros_like(inject)
    fill_padded(faces, tiles, d, pad, grid, hw, he, north, south, corners, polar, link, turn)
    group = 8

    def add_group(i, carry):
        source, at = i // (slots // group), lax.rem(i, slots // group) * group

        @pl.when(cells[source, at] < cell_total)
        def _():
            chunk = encoded[pl.ds(pl.multiple_of(i * group, group), group)]
            for j in range(group):
                place = cells[source, at + j]
                inject[pl.ds(place, 1)] += chunk[j : j + 1]

        return carry

    lax.fori_loop(0, sources * slots // group, add_group, 0)

    def step(i, carry):
        start = i * step_rows
        first = jax.nn.gelu(
            conv_rows(pad, wide_taps, bias, d, start, step_rows, cols), approximate=True
        )
        at = pl.multiple_of(start * cols, step_rows * cols)
        added = inject[pl.ds(at, step_rows * cols)].reshape(step_rows, cols, channels)
        mixed[pl.ds(start, step_rows)] = (first + added).astype(jnp.bfloat16)
        return carry

    lax.fori_loop(0, rows // step_rows, step, 0)
    pw_out[...] = pack_columns(mixed[:, :EDGE].astype(jnp.float32), d_next, False)
    pe_out[...] = pack_columns(mixed[:, cols - EDGE :].astype(jnp.float32), d_next, True)


def second_compute_kernel(
    faces, tiles, d, step_rows,
    link, turn, grid, hw, he, north, south, corners, polar, taps, bias, fields,
    out, pad, wide_taps,
):
    rows, cols = grid.shape[0], grid.shape[1]
    fill_taps(taps, wide_taps)
    fill_padded(faces, tiles, d, pad, grid, hw, he, north, south, corners, polar, link, turn)

    def step(i, carry):
        start = i * step_rows
        second = jax.nn.gelu(
            conv_rows(pad, wide_taps, bias, d, start, step_rows, cols), approximate=True
        )
        here = fields[pl.ds(start, step_rows)].astype(jnp.float32)
        out[pl.ds(start, step_rows)] = (here + second).astype(jnp.bfloat16)
        return carry

    lax.fori_loop(0, rows // step_rows, step, 0)


def local(
    fields, first_kernel_taps, first_conv_bias, second_kernel_taps, second_conv_bias,
    obs_weight, obs_values, obs_owner, obs_cells, polar_neighbor_sector, polar_link_reversal,
):
    faces, tiles = lax.axis_size("face"), lax.axis_size("tile")
    rows, cols, channels = fields.shape
    obs_rows, features = obs_values.shape
    dest_count = faces * tiles
    slots = 2 * obs_rows // dest_count
    cell_total = rows * cols
    step_rows = 4
    bf16, f32, i32 = jnp.bfloat16, jnp.float32, jnp.int32
    shape = jax.ShapeDtypeStruct
    vmem = pl.BlockSpec(memory_space=pltpu.VMEM)
    smem = pl.BlockSpec(memory_space=pltpu.SMEM)
    anywhere = pl.BlockSpec(memory_space=pl.ANY)
    params = pltpu.CompilerParams(vmem_limit_bytes=VMEM_LIMIT)

    def packed_shape(d):
        return shape((rows * d // EDGE, EDGE, channels), bf16)

    def halo_shapes(d):
        return [
            packed_shape(d), packed_shape(d),
            shape((d, cols, channels), bf16), shape((d, cols, channels), bf16),
            shape((4, d, EDGE, channels), bf16), shape((faces, d, cols, channels), bf16),
        ]

    halo_copies = 8 + 2 * (faces - 1)
    dma = pltpu.SemaphoreType.DMA
    d1, d2 = FIRST_DILATION, SECOND_DILATION

    def edge_block(index):
        return pl.BlockSpec((rows, EDGE, channels), lambda i: (0, index, 0))

    whole = lambda *dims: pl.BlockSpec(dims, lambda i: (0,) * len(dims))
    send_rows, send_cells, pw, pe = pl.pallas_call(
        functools.partial(pack_kernel, dest_count, slots, cell_total, d1),
        grid=(1,),
        out_shape=[
            shape((dest_count, slots, features), bf16), shape((dest_count, 1, LANES), i32),
            packed_shape(d1), packed_shape(d1),
        ],
        in_specs=[
            whole(1, obs_rows), whole(1, obs_rows), whole(obs_rows, features),
            edge_block(0), edge_block(cols // EDGE - 1),
        ],
        out_specs=[
            whole(dest_count, slots, features), whole(dest_count, 1, LANES),
            whole(*packed_shape(d1).shape), whole(*packed_shape(d1).shape),
        ],
        compiler_params=params,
        name="pack_observations",
    )(obs_owner.reshape(1, obs_rows), obs_cells.reshape(1, obs_rows), obs_values, fields, fields)

    *halo, recv_rows, recv_cells = pl.pallas_call(
        functools.partial(first_exchange_kernel, faces, tiles, d1),
        out_shape=halo_shapes(d1) + [
            shape((dest_count, slots, features), bf16), shape((dest_count, 1, LANES), i32),
        ],
        in_specs=[anywhere] * 5,
        out_specs=[anywhere] * 8,
        scratch_shapes=[
            dma((halo_copies,)), dma((halo_copies,)), dma((dest_count,)), dma((dest_count,)),
            dma((dest_count,)), dma((dest_count,)), dma((3,)),
        ],
        compiler_params=pltpu.CompilerParams(collective_id=0, has_side_effects=True),
        name="first_exchange",
    )(fields, pw, pe, send_rows, send_cells)

    mixed, pw, pe = pl.pallas_call(
        functools.partial(first_compute_kernel, faces, tiles, d1, d2, step_rows),
        out_shape=[shape((rows, cols, channels), bf16), packed_shape(d2), packed_shape(d2)],
        in_specs=[smem] * 3 + [vmem] * 11,
        out_specs=[vmem] * 3,
        scratch_shapes=[
            pltpu.VMEM((rows + 2 * d1, cols + EDGE, channels), bf16),
            pltpu.VMEM((3 * channels, 3 * channels), bf16),
            pltpu.VMEM((cell_total + 8, channels), f32),
            pltpu.VMEM((dest_count * slots, channels), f32),
        ],
        compiler_params=params,
        name="first_compute",
    )(
        polar_neighbor_sector, polar_link_reversal, recv_cells.reshape(dest_count, LANES),
        fields, *halo, first_kernel_taps, first_conv_bias.reshape(1, channels), recv_rows, obs_weight,
    )

    halo = pl.pallas_call(
        functools.partial(second_exchange_kernel, faces, tiles, d2),
        out_shape=halo_shapes(d2),
        in_specs=[anywhere] * 3,
        out_specs=[anywhere] * 6,
        scratch_shapes=[dma((halo_copies,)), dma((halo_copies,)), dma((1,))],
        compiler_params=pltpu.CompilerParams(collective_id=1, has_side_effects=True),
        name="second_exchange",
    )(mixed, pw, pe)

    return pl.pallas_call(
        functools.partial(second_compute_kernel, faces, tiles, d2, step_rows),
        out_shape=shape((rows, cols, channels), bf16),
        in_specs=[smem] * 2 + [vmem] * 10,
        out_specs=vmem,
        scratch_shapes=[
            pltpu.VMEM((rows + 2 * d2, cols + EDGE, channels), bf16),
            pltpu.VMEM((3 * channels, 3 * channels), bf16),
        ],
        compiler_params=params,
        name="second_compute",
    )(
        polar_neighbor_sector, polar_link_reversal,
        mixed, *halo, second_kernel_taps, second_conv_bias.reshape(1, channels), fields,
    )


def solution(mesh):
    in_specs = (
        P("tile", "face", None), P(), P(), P(), P(), P(),
        P(("face", "tile"), None), P(("face", "tile"), None), P(("face", "tile")), P(), P(),
    )
    return jax.shard_map(
        local, mesh=mesh, in_specs=in_specs, out_specs=P("tile", "face", None), check_vma=False
    )
```

```python
import functools

import jax
import jax.numpy as jnp
from jax import lax
from jax.experimental import pallas as pl
from jax.experimental.pallas import tpu as pltpu
from jax.sharding import PartitionSpec as P

FIRST_DILATION = 2
SECOND_DILATION = 4
MESH = pl.DeviceIdType.MESH
LANES = 128
EDGE = 16
STEP = 8
VMEM_LIMIT = 56 * 1024 * 1024


def pack_columns(tile, d, east):
    rows, _, ch = tile.shape
    per = 8 // d
    half = tile[:, 8:] if east else tile[:, :8]
    grouped = half.reshape(rows // per, per, 8, ch)
    sub = lax.broadcasted_iota(jnp.int32, (rows // per, 8, ch), 1)
    out = None
    for j in range(per):
        shift = (j * d - (8 - d if east else 0)) % 8
        part = grouped[:, j]
        if shift:
            part = pltpu.roll(part, shift, 1)
        out = part if out is None else jnp.where(sub >= j * d, part, out)
    return out.reshape(rows // (2 * per), EDGE, ch).astype(jnp.bfloat16)


def unpack_columns(packed, d, west):
    count, _, ch = packed.shape
    per = 8 // d
    pieces = packed.astype(jnp.float32).reshape(2 * count, 8, ch)
    parts = []
    for j in range(per):
        shift = ((8 - d if west else 0) - j * d) % 8
        parts.append(pltpu.roll(pieces, shift, 1) if shift else pieces)
    return jnp.stack(parts, axis=1).reshape(2 * count * per, 8, ch)


def join_edge(east_tile, west_tile):
    east = east_tile.astype(jnp.float32)
    west = west_tile.astype(jnp.float32)
    axis = east.ndim - 2
    return jnp.concatenate(
        [lax.slice_in_dim(east, 0, 8, axis=axis), lax.slice_in_dim(west, 8, 16, axis=axis)], axis=axis
    ).astype(jnp.bfloat16)


def pack_observations(dest_count, slots, cell_total, owner_ref, cells_ref, values_ref, rows_out, cells_out):
    obs = owner_ref.shape[1]
    owner = owner_ref[...]
    dests = lax.broadcasted_iota(jnp.int32, (dest_count, obs), 0)
    onehot = jnp.where(dests == owner, 1.0, 0.0)
    before = (
        lax.broadcasted_iota(jnp.int32, (obs, obs), 0) < lax.broadcasted_iota(jnp.int32, (obs, obs), 1)
    )
    ranks = jnp.dot(
        onehot.astype(jnp.bfloat16),
        jnp.where(before, 1.0, 0.0).astype(jnp.bfloat16),
        preferred_element_type=jnp.float32,
    )
    rank = jnp.sum(ranks * onehot, axis=0, keepdims=True).astype(jnp.int32)
    target = owner * slots + rank
    cells = cells_ref[...]
    kind = lax.broadcasted_iota(jnp.int32, (8, obs), 0)
    codes = jnp.where(kind == 0, cells >> 7, jnp.where(kind == 1, cells & 127, 1))
    codes = codes.astype(jnp.float32).astype(jnp.bfloat16)
    values = values_ref[...]
    cells_out[...] = jnp.full(cells_out.shape, cell_total, jnp.int32)
    block = min(512, dest_count * slots)
    for base in range(0, dest_count * slots, block):
        wanted = base + lax.broadcasted_iota(jnp.int32, (block, obs), 0)
        match = jnp.where(wanted == target, 1.0, 0.0).astype(jnp.bfloat16)
        rows = jnp.dot(match, values, preferred_element_type=jnp.float32).astype(jnp.bfloat16)
        first = base // slots
        rows_out[first : first + block // slots] = rows.reshape(block // slots, slots, rows.shape[-1])
        got = lax.dot_general(
            codes, match, (((1,), (1,)), ((), ())), preferred_element_type=jnp.float32
        )
        found = (got[0:1] * LANES + got[1:2]).astype(jnp.int32)
        found = jnp.where(got[2:3] > 0.5, found, cell_total)
        for j in range(block // slots):
            cells_out[first + j, :, :slots] = found[:, j * slots : (j + 1) * slots]


def halo_sends(faces, tiles, d, grid, pw, pe, hw, he, north, south, corners, polar):
    s, t = lax.axis_index("face"), lax.axis_index("tile")
    rows, cols = grid.shape[0], grid.shape[1]
    east, west = lax.rem(s + 1, faces), lax.rem(s + faces - 1, faces)
    last, first = pl.ds(rows - d, d), pl.ds(0, d)
    right, left = pl.ds(cols - EDGE, EDGE), pl.ds(0, EDGE)
    not_top, not_low = t > 0, t < tiles - 1
    up, down = t - 1, t + 1
    plan = [
        (None, None, pe, hw, (east, t)),
        (None, None, pw, he, (west, t)),
        (not_low, not_top, grid.at[last], north, (s, down)),
        (not_top, not_low, grid.at[first], south, (s, up)),
        (not_low, not_top, grid.at[last, right], corners.at[0], (east, down)),
        (not_low, not_top, grid.at[last, left], corners.at[1], (west, down)),
        (not_top, not_low, grid.at[first, right], corners.at[2], (east, up)),
        (not_top, not_low, grid.at[first, left], corners.at[3], (west, up)),
    ]
    for k in range(1, faces):
        to = (lax.rem(s + k, faces), t)
        plan.append((t == 0, t == 0, grid.at[first], polar.at[s], to))
    for k in range(1, faces):
        to = (lax.rem(s + k, faces), t)
        plan.append((t == tiles - 1, t == tiles - 1, grid.at[last], polar.at[s], to))
    return plan


def guarded(cond, action):
    if cond is None:
        action()
    else:
        pl.when(cond)(action)


def start_halo(plan, send_sem, recv_sem):
    copies = []
    for i, (sends, receives, src, dst, to) in enumerate(plan):
        copy = pltpu.make_async_remote_copy(
            src_ref=src, dst_ref=dst, send_sem=send_sem.at[i], recv_sem=recv_sem.at[i],
            device_id=to, device_id_type=MESH,
        )
        guarded(sends, copy.start)
        copies.append((sends, receives, copy))
    return copies


def wait_received(copies):
    for _, receives, copy in copies:
        guarded(receives, copy.wait_recv)


def wait_sent(copies):
    for sends, _, copy in copies:
        guarded(sends, copy.wait_send)


def own_polar(grid, polar, d, tiles, sem):
    s, t = lax.axis_index("face"), lax.axis_index("tile")
    top = pltpu.make_async_copy(grid.at[pl.ds(0, d)], polar.at[s], sem)
    low = pltpu.make_async_copy(grid.at[pl.ds(grid.shape[0] - d, d)], polar.at[s], sem)
    return [(t == 0, top), (t == tiles - 1, low)]


def fill_columns(d, pad, rows, cols, hw, he):
    pad[d : d + rows, cols:] = jnp.concatenate(
        [unpack_columns(he[...], d, False), unpack_columns(hw[...], d, True)], axis=1
    ).astype(jnp.bfloat16)


def fill_ends(faces, tiles, d, pad, rows, cols, north, south, corners, polar, link, turn):
    s, t = lax.axis_index("face"), lax.axis_index("tile")
    wide = cols + EDGE

    def from_pole(base, column):
        p = link[column, s]
        east, west = lax.rem(p + 1, faces), lax.rem(p + faces - 1, faces)
        here = lax.broadcasted_iota(jnp.int32, (wide, wide), 0)
        there = lax.broadcasted_iota(jnp.int32, (wide, wide), 1)
        mirrored = jnp.where(here < cols, cols - 1 - here, wide + cols - 1 - here)
        source = jnp.where(turn[column, s] == 1, mirrored, here)
        move = jnp.where(there == source, 1.0, 0.0).astype(jnp.bfloat16)
        for i in range(d):
            k = d - 1 - i
            edge = join_edge(polar[east, k, :EDGE], polar[west, k, cols - EDGE :])
            line = jnp.concatenate([polar[p, k], edge], axis=0)
            pad[base + i] = jnp.dot(move, line, preferred_element_type=jnp.float32).astype(jnp.bfloat16)

    @pl.when(t == 0)
    def _():
        from_pole(0, 0)

    @pl.when(t > 0)
    def _():
        pad[:d, :cols] = north[...]
        pad[:d, cols:] = join_edge(corners[1], corners[0])

    @pl.when(t == tiles - 1)
    def _():
        from_pole(d + rows, 1)

    @pl.when(t < tiles - 1)
    def _():
        pad[d + rows :, :cols] = south[...]
        pad[d + rows :, cols:] = join_edge(corners[3], corners[2])


def fill_taps(taps, wide_taps):
    channels, features = taps.shape[1], taps.shape[2]
    for k in range(4):
        for e in range(3):
            for j in range(2):
                piece = (
                    taps[3 * (k - j) + e] if 0 <= k - j <= 2 else jnp.zeros((channels, features), jnp.bfloat16)
                )
                at = (2 * e + j) * features
                wide_taps[k * channels : (k + 1) * channels, at : at + features] = piece


def conv_rows(pad, wide_taps, bias, d, start, cols):
    wide = cols + EDGE
    features = bias.shape[-1]
    count = STEP // (2 * d)
    lines = []
    for k in range(4):
        blocks = [pad[pl.ds(start + m * 2 * d + k * d, d)] for m in range(count)]
        lines.append(jnp.concatenate(blocks, axis=0).reshape(count * d * wide, pad.shape[-1]))
    product = jnp.dot(
        jnp.concatenate(lines, axis=1), wide_taps[...], preferred_element_type=jnp.float32
    ).reshape(count * d, wide, 6 * features)
    halves = []
    for j in range(2):
        low, middle, high = (
            product[:, :, (2 * e + j) * features : (2 * e + j + 1) * features] for e in range(3)
        )
        total = pltpu.roll(low, d, 1) + middle + pltpu.roll(high, wide - d, 1)
        halves.append(total[:, :cols] + bias[...].reshape(1, 1, features))
    return [(m * 2 * d + j * d, halves[j][m * d : (m + 1) * d]) for m in range(count) for j in range(2)]


def first_kernel(
    faces, tiles, d, slots,
    link, turn, owner, cells, values, taps, bias, grid,
    first, rows_in, cells_in,
    pad, wide_taps, held, rows_out, cells_out, pw, pe, hw, he, north, south, corners, polar,
    send_sem, recv_sem, row_send, row_recv, cell_send, cell_recv, own_sem,
):
    rows, cols, channels = grid.shape
    cell_total = rows * cols
    count = faces * tiles
    me = lax.axis_index("face") * tiles + lax.axis_index("tile")
    barrier = pltpu.get_barrier_semaphore()
    load = pltpu.make_async_copy(grid, pad.at[pl.ds(d, rows), pl.ds(0, cols)], own_sem.at[3])
    load.start()

    def device(k):
        other = lax.rem(me + k, count)
        return other, (other // tiles, lax.rem(other, tiles))

    def greet(k, carry):
        _, to = device(k)
        pl.semaphore_signal(barrier, inc=1, device_id=to, device_id_type=MESH)
        return carry

    lax.fori_loop(1, count, greet, 0)
    own = own_polar(grid, polar, d, tiles, own_sem.at[2])
    for cond, copy in own:
        guarded(cond, copy.start)
    load.wait()
    pw[...] = pack_columns(pad[d : d + rows, :EDGE].astype(jnp.float32), d, False)
    pe[...] = pack_columns(pad[d : d + rows, cols - EDGE : cols].astype(jnp.float32), d, True)
    pl.semaphore_wait(barrier, count - 1)
    copies = start_halo(
        halo_sends(faces, tiles, d, grid, pw, pe, hw, he, north, south, corners, polar), send_sem, recv_sem
    )

    pack_observations(count, slots, cell_total, owner, cells, values, rows_out, cells_out)

    def row_copy(k):
        other, to = device(k)
        return pltpu.make_async_remote_copy(
            src_ref=rows_out.at[other], dst_ref=rows_in.at[me],
            send_sem=row_send.at[k], recv_sem=row_recv.at[k], device_id=to, device_id_type=MESH,
        )

    def cell_copy(k):
        other, to = device(k)
        return pltpu.make_async_remote_copy(
            src_ref=cells_out.at[other], dst_ref=cells_in.at[me],
            send_sem=cell_send.at[k], recv_sem=cell_recv.at[k], device_id=to, device_id_type=MESH,
        )

    def send(k, carry):
        row_copy(k).start()
        cell_copy(k).start()
        return carry

    def finish(k, carry):
        row_copy(k).wait()
        cell_copy(k).wait()
        return carry

    lax.fori_loop(1, count, send, 0)
    own_rows = pltpu.make_async_copy(rows_out.at[me], rows_in.at[me], own_sem.at[0])
    own_cells = pltpu.make_async_copy(cells_out.at[me], cells_in.at[me], own_sem.at[1])
    own_rows.start()
    own_cells.start()

    fill_taps(taps, wide_taps)
    wait_received(copies[:2])
    fill_columns(d, pad, rows, cols, hw, he)

    def step(i, carry):
        start = i * STEP
        for offset, piece in conv_rows(pad, wide_taps, bias, d, start, cols):
            at = pl.multiple_of((start + offset) * cols, d * cols)
            held[pl.ds(at, d * cols)] = jax.nn.gelu(piece, approximate=True).reshape(d * cols, channels)
        return carry

    steps = rows // STEP
    lax.fori_loop(1, steps - 1, step, 0, unroll=2)
    wait_received(copies[2:])
    for cond, copy in own:
        guarded(cond, copy.wait)
    fill_ends(faces, tiles, d, pad, rows, cols, north, south, corners, polar, link, turn)
    step(0, 0)
    step(steps - 1, 0)
    store = pltpu.make_async_copy(held, first, own_sem.at[4])
    store.start()
    wait_sent(copies)
    own_rows.wait()
    own_cells.wait()
    lax.fori_loop(1, count, finish, 0)
    store.wait()


def inject_kernel(d_next, cells, first, values, weight, mixed, pw_out, pe_out, total, encoded, sem):
    rows, cols, channels = mixed.shape
    sources, slots, features = values.shape
    cell_total = rows * cols
    load = pltpu.make_async_copy(first, total.at[pl.ds(0, cell_total)], sem)
    load.start()
    encoded[...] = jnp.dot(
        values[...].reshape(sources * slots, features), weight[...], preferred_element_type=jnp.float32
    )
    total[cell_total:] = jnp.zeros((total.shape[0] - cell_total, channels), jnp.float32)
    load.wait()
    group = 8

    def add_group(i, carry):
        source, at = i // (slots // group), lax.rem(i, slots // group) * group

        @pl.when(cells[source, at] < cell_total)
        def _():
            chunk = encoded[pl.ds(pl.multiple_of(i * group, group), group)]
            for j in range(group):
                place = cells[source, at + j]
                total[pl.ds(place, 1)] += chunk[j : j + 1]

        return carry

    lax.fori_loop(0, sources * slots // group, add_group, 0)

    def step(i, carry):
        at = pl.multiple_of(i * STEP * cols, STEP * cols)
        here = total[pl.ds(at, STEP * cols)].reshape(STEP, cols, channels)
        mixed[pl.ds(i * STEP, STEP)] = here.astype(jnp.bfloat16)
        return carry

    lax.fori_loop(0, rows // STEP, step, 0)
    pw_out[...] = pack_columns(mixed[:, :EDGE].astype(jnp.float32), d_next, False)
    pe_out[...] = pack_columns(mixed[:, cols - EDGE :].astype(jnp.float32), d_next, True)


def second_kernel(
    faces, tiles, d, link, turn, taps, bias, grid, pw, pe, fields,
    out,
    pad, wide_taps, held, hw, he, north, south, corners, polar, send_sem, recv_sem, own_sem,
):
    rows, cols, channels = grid.shape
    s, t = lax.axis_index("face"), lax.axis_index("tile")
    barrier = pltpu.get_barrier_semaphore()

    def greet(to):
        pl.semaphore_signal(barrier, inc=1, device_id=to, device_id_type=MESH)

    east, west = lax.rem(s + 1, faces), lax.rem(s + faces - 1, faces)
    greet((east, t))
    greet((west, t))

    @pl.when(t > 0)
    def _():
        for f in (east, s, west):
            greet((f, t - 1))

    @pl.when(t < tiles - 1)
    def _():
        for f in (east, s, west):
            greet((f, t + 1))

    polar_end = (t == 0) | (t == tiles - 1)

    @pl.when(polar_end)
    def _():
        for k in range(2, faces - 1):
            greet((lax.rem(s + k, faces), t))

    own = own_polar(grid, polar, d, tiles, own_sem.at[0])
    for cond, copy in own:
        guarded(cond, copy.start)
    load = pltpu.make_async_copy(grid, pad.at[pl.ds(d, rows), pl.ds(0, cols)], own_sem.at[1])
    load.start()
    load_fields = pltpu.make_async_copy(fields, held, own_sem.at[2])
    load_fields.start()

    @pl.when(polar_end)
    def _():
        pl.semaphore_wait(barrier, 5 + faces - 3)

    @pl.when(jnp.logical_not(polar_end))
    def _():
        pl.semaphore_wait(barrier, 8)

    copies = start_halo(
        halo_sends(faces, tiles, d, grid, pw, pe, hw, he, north, south, corners, polar), send_sem, recv_sem
    )
    fill_taps(taps, wide_taps)
    load.wait()
    load_fields.wait()
    wait_received(copies[:2])
    fill_columns(d, pad, rows, cols, hw, he)

    def step(i, carry):
        start = i * STEP
        for offset, piece in conv_rows(pad, wide_taps, bias, d, start, cols):
            here = held[pl.ds(start + offset, d)].astype(jnp.float32)
            out[pl.ds(start + offset, d)] = (
                here + jax.nn.gelu(piece, approximate=True)
            ).astype(jnp.bfloat16)
        return carry

    steps = rows // STEP
    lax.fori_loop(1, steps - 1, step, 0, unroll=2)
    wait_received(copies[2:])
    for cond, copy in own:
        guarded(cond, copy.wait)
    fill_ends(faces, tiles, d, pad, rows, cols, north, south, corners, polar, link, turn)
    step(0, 0)
    step(steps - 1, 0)
    wait_sent(copies)


def local(
    fields, first_kernel_taps, first_conv_bias, second_kernel_taps, second_conv_bias,
    obs_weight, obs_values, obs_owner, obs_cells, polar_neighbor_sector, polar_link_reversal,
):
    faces, tiles = lax.axis_size("face"), lax.axis_size("tile")
    rows, cols, channels = fields.shape
    obs_rows, features = obs_values.shape
    dest_count = faces * tiles
    slots = 2 * obs_rows // dest_count
    cell_total = rows * cols
    bf16, f32, i32 = jnp.bfloat16, jnp.float32, jnp.int32
    shape = jax.ShapeDtypeStruct
    vmem = pl.BlockSpec(memory_space=pltpu.VMEM)
    smem = pl.BlockSpec(memory_space=pltpu.SMEM)
    anywhere = pl.BlockSpec(memory_space=pl.ANY)
    dma = pltpu.SemaphoreType.DMA
    d1, d2 = FIRST_DILATION, SECOND_DILATION
    halo_copies = 8 + 2 * (faces - 1)
    link, turn = polar_neighbor_sector.T, polar_link_reversal.T

    def packed_dims(d):
        return (rows * d // EDGE, EDGE, channels)

    def conv_scratch(d):
        return [
            pltpu.VMEM((rows + 2 * d, cols + EDGE, channels), bf16),
            pltpu.VMEM((4 * channels, 6 * channels), bf16),
        ]

    def halo_scratch(d):
        return [
            pltpu.VMEM(packed_dims(d), bf16), pltpu.VMEM(packed_dims(d), bf16),
            pltpu.VMEM((d, cols, channels), bf16), pltpu.VMEM((d, cols, channels), bf16),
            pltpu.VMEM((4, d, EDGE, channels), bf16), pltpu.VMEM((faces, d, cols, channels), bf16),
        ]

    first, recv_rows, recv_cells = pl.pallas_call(
        functools.partial(first_kernel, faces, tiles, d1, slots),
        out_shape=[
            shape((cell_total, channels), f32),
            shape((dest_count, slots, features), bf16),
            shape((dest_count, 1, LANES), i32),
        ],
        in_specs=[smem] * 2 + [vmem] * 5 + [anywhere],
        out_specs=[anywhere] * 3,
        scratch_shapes=conv_scratch(d1) + [
            pltpu.VMEM((cell_total, channels), f32),
            pltpu.VMEM((dest_count, slots, features), bf16),
            pltpu.VMEM((dest_count, 1, LANES), i32),
            pltpu.VMEM(packed_dims(d1), bf16), pltpu.VMEM(packed_dims(d1), bf16),
        ] + halo_scratch(d1) + [
            dma((halo_copies,)), dma((halo_copies,)), dma((dest_count,)), dma((dest_count,)),
            dma((dest_count,)), dma((dest_count,)), dma((5,)),
        ],
        compiler_params=pltpu.CompilerParams(
            collective_id=0, has_side_effects=True, vmem_limit_bytes=VMEM_LIMIT
        ),
        name="first_conv_and_exchange",
    )(
        link, turn, obs_owner.reshape(1, obs_rows), obs_cells.reshape(1, obs_rows), obs_values,
        first_kernel_taps, first_conv_bias.reshape(1, channels), fields,
    )

    mixed, pw, pe = pl.pallas_call(
        functools.partial(inject_kernel, d2),
        out_shape=[
            shape((rows, cols, channels), bf16), shape(packed_dims(d2), bf16), shape(packed_dims(d2), bf16)
        ],
        in_specs=[smem, anywhere, vmem, vmem],
        out_specs=[vmem] * 3,
        scratch_shapes=[
            pltpu.VMEM((cell_total + 8, channels), f32),
            pltpu.VMEM((dest_count * slots, channels), f32),
            dma,
        ],
        compiler_params=pltpu.CompilerParams(vmem_limit_bytes=VMEM_LIMIT),
        name="inject",
    )(recv_cells.reshape(dest_count, LANES), first, recv_rows, obs_weight)

    return pl.pallas_call(
        functools.partial(second_kernel, faces, tiles, d2),
        out_shape=shape((rows, cols, channels), bf16),
        in_specs=[smem] * 2 + [vmem] * 2 + [anywhere] * 4,
        out_specs=vmem,
        scratch_shapes=conv_scratch(d2) + [pltpu.VMEM((rows, cols, channels), bf16)]
        + halo_scratch(d2) + [dma((halo_copies,)), dma((halo_copies,)), dma((3,))],
        compiler_params=pltpu.CompilerParams(
            collective_id=1, has_side_effects=True, vmem_limit_bytes=VMEM_LIMIT
        ),
        name="second_conv_and_exchange",
    )(
        link, turn, second_kernel_taps, second_conv_bias.reshape(1, channels), mixed, pw, pe, fields
    )


def solution(mesh):
    in_specs = (
        P("tile", "face", None), P(), P(), P(), P(), P(),
        P(("face", "tile"), None), P(("face", "tile"), None), P(("face", "tile")), P(), P(),
    )
    return jax.shard_map(
        local, mesh=mesh, in_specs=in_specs, out_specs=P("tile", "face", None), check_vma=False
    )
```

```python
import functools

import jax
import jax.numpy as jnp
from jax import lax
from jax.experimental import pallas as pl
from jax.experimental.pallas import tpu as pltpu
from jax.sharding import PartitionSpec as P

FIRST_DILATION = 2
SECOND_DILATION = 4
MESH = pl.DeviceIdType.MESH
LANES = 128
EDGE = 16
STEP = 8
GROUP = 8
REPEAT = 1 << 14
VMEM_LIMIT = 56 * 1024 * 1024


def pack_columns(tile, d, east):
    rows, _, ch = tile.shape
    per = 8 // d
    half = tile[:, 8:] if east else tile[:, :8]
    grouped = half.reshape(rows // per, per, 8, ch)
    sub = lax.broadcasted_iota(jnp.int32, (rows // per, 8, ch), 1)
    out = None
    for j in range(per):
        shift = (j * d - (8 - d if east else 0)) % 8
        part = grouped[:, j]
        if shift:
            part = pltpu.roll(part, shift, 1)
        out = part if out is None else jnp.where(sub >= j * d, part, out)
    return out.reshape(rows // (2 * per), EDGE, ch).astype(jnp.bfloat16)


def unpack_columns(packed, d, west):
    count, _, ch = packed.shape
    per = 8 // d
    pieces = packed.astype(jnp.float32).reshape(2 * count, 8, ch)
    parts = []
    for j in range(per):
        shift = ((8 - d if west else 0) - j * d) % 8
        parts.append(pltpu.roll(pieces, shift, 1) if shift else pieces)
    return jnp.stack(parts, axis=1).reshape(2 * count * per, 8, ch)


def join_edge(east_tile, west_tile):
    east = east_tile.astype(jnp.float32)
    west = west_tile.astype(jnp.float32)
    axis = east.ndim - 2
    return jnp.concatenate(
        [lax.slice_in_dim(east, 0, 8, axis=axis), lax.slice_in_dim(west, 8, 16, axis=axis)], axis=axis
    ).astype(jnp.bfloat16)


def rank_observations(dest_count, slots, owner_ref, cells_ref):
    obs = owner_ref.shape[1]
    owner = owner_ref[...]
    dests = lax.broadcasted_iota(jnp.int32, (dest_count, obs), 0)
    onehot = jnp.where(dests == owner, 1.0, 0.0)
    before = (
        lax.broadcasted_iota(jnp.int32, (obs, obs), 0) < lax.broadcasted_iota(jnp.int32, (obs, obs), 1)
    )
    ranks = jnp.dot(
        onehot.astype(jnp.bfloat16),
        jnp.where(before, 1.0, 0.0).astype(jnp.bfloat16),
        preferred_element_type=jnp.float32,
    )
    rank = jnp.sum(ranks * onehot, axis=0, keepdims=True).astype(jnp.int32)
    target = owner * slots + rank
    cells = cells_ref[...]
    kind = lax.broadcasted_iota(jnp.int32, (8, obs), 0)
    codes = jnp.where(kind == 0, cells >> 7, jnp.where(kind == 1, cells & 127, 1))
    codes = codes.astype(jnp.float32).astype(jnp.bfloat16)
    return target, codes


def pack_block(block, slots, cell_total, face, target, codes, values, rows_out, cells_out):
    obs = target.shape[1]
    first = face * (block // slots)
    wanted = face * block + lax.broadcasted_iota(jnp.int32, (block, obs), 0)
    match = jnp.where(wanted == target, 1.0, 0.0).astype(jnp.bfloat16)
    rows = jnp.dot(match, values[...], preferred_element_type=jnp.float32).astype(jnp.bfloat16)
    rows_out[pl.ds(first, block // slots)] = rows.reshape(block // slots, slots, rows.shape[-1])
    got = lax.dot_general(codes, match, (((1,), (1,)), ((), ())), preferred_element_type=jnp.float32)
    found = (got[0:1] * LANES + got[1:2]).astype(jnp.int32)
    found = jnp.broadcast_to(jnp.where(got[2:3] > 0.5, found, cell_total), (8, block))
    place = lax.broadcasted_iota(jnp.int32, (8, block), 1) & (GROUP - 1)
    repeats = jnp.zeros((8, block), jnp.int32)
    for k in range(1, GROUP):
        same = (found == pltpu.roll(found, k, 1)) & (place >= k) & (found < cell_total)
        repeats = jnp.where(same, REPEAT, repeats)
    found = found + repeats
    for j in range(block // slots):
        cells_out[first + j, :, :slots] = found[:1, j * slots : (j + 1) * slots]


def halo_sends(faces, tiles, d, grid, pw, pe, hw, he, north, south, corners, polar):
    s, t = lax.axis_index("face"), lax.axis_index("tile")
    rows, cols = grid.shape[0], grid.shape[1]
    east, west = lax.rem(s + 1, faces), lax.rem(s + faces - 1, faces)
    last, first = pl.ds(rows - d, d), pl.ds(0, d)
    right, left = pl.ds(cols - EDGE, EDGE), pl.ds(0, EDGE)
    not_top, not_low = t > 0, t < tiles - 1
    up, down = t - 1, t + 1
    plan = [
        (None, None, pe, hw, (east, t)),
        (None, None, pw, he, (west, t)),
        (not_low, not_top, grid.at[last], north, (s, down)),
        (not_top, not_low, grid.at[first], south, (s, up)),
        (not_low, not_top, grid.at[last, right], corners.at[0], (east, down)),
        (not_low, not_top, grid.at[last, left], corners.at[1], (west, down)),
        (not_top, not_low, grid.at[first, right], corners.at[2], (east, up)),
        (not_top, not_low, grid.at[first, left], corners.at[3], (west, up)),
    ]
    for k in range(1, faces):
        to = (lax.rem(s + k, faces), t)
        plan.append((t == 0, t == 0, grid.at[first], polar.at[s], to))
    for k in range(1, faces):
        to = (lax.rem(s + k, faces), t)
        plan.append((t == tiles - 1, t == tiles - 1, grid.at[last], polar.at[s], to))
    return plan


def guarded(cond, action):
    if cond is None:
        action()
    else:
        pl.when(cond)(action)


def start_halo(plan, send_sem, recv_sem):
    copies = []
    for i, (sends, receives, src, dst, to) in enumerate(plan):
        copy = pltpu.make_async_remote_copy(
            src_ref=src, dst_ref=dst, send_sem=send_sem.at[i], recv_sem=recv_sem.at[i],
            device_id=to, device_id_type=MESH,
        )
        guarded(sends, copy.start)
        copies.append((sends, receives, copy))
    return copies


def wait_received(copies):
    for _, receives, copy in copies:
        guarded(receives, copy.wait_recv)


def wait_sent(copies):
    for sends, _, copy in copies:
        guarded(sends, copy.wait_send)


def own_polar(grid, polar, d, tiles, sem):
    s, t = lax.axis_index("face"), lax.axis_index("tile")
    top = pltpu.make_async_copy(grid.at[pl.ds(0, d)], polar.at[s], sem)
    low = pltpu.make_async_copy(grid.at[pl.ds(grid.shape[0] - d, d)], polar.at[s], sem)
    return [(t == 0, top), (t == tiles - 1, low)]


def fill_columns(d, pad, rows, cols, hw, he):
    pad[d : d + rows, cols:] = jnp.concatenate(
        [unpack_columns(he[...], d, False), unpack_columns(hw[...], d, True)], axis=1
    ).astype(jnp.bfloat16)


def fill_ends(faces, tiles, d, pad, rows, cols, north, south, corners, polar, link, turn):
    s, t = lax.axis_index("face"), lax.axis_index("tile")
    wide = cols + EDGE

    def from_pole(base, column):
        p = link[column, s]
        east, west = lax.rem(p + 1, faces), lax.rem(p + faces - 1, faces)
        here = lax.broadcasted_iota(jnp.int32, (wide, wide), 0)
        there = lax.broadcasted_iota(jnp.int32, (wide, wide), 1)
        mirrored = jnp.where(here < cols, cols - 1 - here, wide + cols - 1 - here)
        source = jnp.where(turn[column, s] == 1, mirrored, here)
        move = jnp.where(there == source, 1.0, 0.0).astype(jnp.bfloat16)
        for i in range(d):
            k = d - 1 - i
            edge = join_edge(polar[east, k, :EDGE], polar[west, k, cols - EDGE :])
            line = jnp.concatenate([polar[p, k], edge], axis=0)
            pad[base + i] = jnp.dot(move, line, preferred_element_type=jnp.float32).astype(jnp.bfloat16)

    @pl.when(t == 0)
    def _():
        from_pole(0, 0)

    @pl.when(t > 0)
    def _():
        pad[:d, :cols] = north[...]
        pad[:d, cols:] = join_edge(corners[1], corners[0])

    @pl.when(t == tiles - 1)
    def _():
        from_pole(d + rows, 1)

    @pl.when(t < tiles - 1)
    def _():
        pad[d + rows :, :cols] = south[...]
        pad[d + rows :, cols:] = join_edge(corners[3], corners[2])


def fill_taps(taps, wide_taps):
    channels, features = taps.shape[1], taps.shape[2]
    for k in range(4):
        for e in range(3):
            for j in range(2):
                piece = (
                    taps[3 * (k - j) + e] if 0 <= k - j <= 2 else jnp.zeros((channels, features), jnp.bfloat16)
                )
                at = (2 * e + j) * features
                wide_taps[k * channels : (k + 1) * channels, at : at + features] = piece


def conv_rows(pad, wide_taps, bias, d, start, cols):
    wide = cols + EDGE
    features = bias.shape[-1]
    count = STEP // (2 * d)
    lines = []
    for k in range(4):
        blocks = [pad[pl.ds(start + m * 2 * d + k * d, d)] for m in range(count)]
        lines.append(jnp.concatenate(blocks, axis=0).reshape(count * d * wide, pad.shape[-1]))
    product = jnp.dot(
        jnp.concatenate(lines, axis=1), wide_taps[...], preferred_element_type=jnp.float32
    ).reshape(count * d, wide, 6 * features)
    halves = []
    for j in range(2):
        low, middle, high = (
            product[:, :, (2 * e + j) * features : (2 * e + j + 1) * features] for e in range(3)
        )
        total = pltpu.roll(low, d, 1) + middle + pltpu.roll(high, wide - d, 1)
        halves.append(total[:, :cols] + bias[...].reshape(1, 1, features))
    return [(m * 2 * d + j * d, halves[j][m * d : (m + 1) * d]) for m in range(count) for j in range(2)]


def first_kernel(
    faces, tiles, d, slots,
    link, turn, owner, cells, values, taps, bias, grid,
    first, rows_in, cells_in,
    pad, wide_taps, held, rows_out, cells_out, pw, pe, hw, he, north, south, corners, polar,
    send_sem, recv_sem, row_send, row_recv, cell_send, cell_recv, own_sem,
):
    rows, cols, channels = grid.shape
    cell_total = rows * cols
    count = faces * tiles
    me = lax.axis_index("face") * tiles + lax.axis_index("tile")
    barrier = pltpu.get_barrier_semaphore()
    load = pltpu.make_async_copy(grid, pad.at[pl.ds(d, rows), pl.ds(0, cols)], own_sem.at[3])
    load.start()

    def device(k):
        other = lax.rem(me + k, count)
        return other, (other // tiles, lax.rem(other, tiles))

    def greet(k, carry):
        _, to = device(k)
        pl.semaphore_signal(barrier, inc=1, device_id=to, device_id_type=MESH)
        return carry

    lax.fori_loop(1, count, greet, 0)
    own = own_polar(grid, polar, d, tiles, own_sem.at[2])
    for cond, copy in own:
        guarded(cond, copy.start)
    cells_out[...] = jnp.full(cells_out.shape, cell_total, jnp.int32)
    target, codes = rank_observations(count, slots, owner, cells)
    load.wait()
    pw[...] = pack_columns(pad[d : d + rows, :EDGE].astype(jnp.float32), d, False)
    pe[...] = pack_columns(pad[d : d + rows, cols - EDGE : cols].astype(jnp.float32), d, True)
    pl.semaphore_wait(barrier, count - 1)
    copies = start_halo(
        halo_sends(faces, tiles, d, grid, pw, pe, hw, he, north, south, corners, polar), send_sem, recv_sem
    )

    def row_copy(other):
        to = (other // tiles, lax.rem(other, tiles))
        return pltpu.make_async_remote_copy(
            src_ref=rows_out.at[other], dst_ref=rows_in.at[me],
            send_sem=row_send.at[lax.rem(other + count - me, count)],
            recv_sem=row_recv.at[lax.rem(other + count - me, count)],
            device_id=to, device_id_type=MESH,
        )

    def cell_copy(other):
        to = (other // tiles, lax.rem(other, tiles))
        return pltpu.make_async_remote_copy(
            src_ref=cells_out.at[other], dst_ref=cells_in.at[me],
            send_sem=cell_send.at[lax.rem(other + count - me, count)],
            recv_sem=cell_recv.at[lax.rem(other + count - me, count)],
            device_id=to, device_id_type=MESH,
        )

    def finish(k, carry):
        other = lax.rem(me + k, count)
        row_copy(other).wait()
        cell_copy(other).wait()
        return carry

    s, t = lax.axis_index("face"), lax.axis_index("tile")
    for b in range(1, faces + 1):
        face = lax.rem(s + b, faces)
        pack_block(tiles * slots, slots, cell_total, face, target, codes, values, rows_out, cells_out)

        def send(k, carry, face=face):
            other = face * tiles + lax.rem(t + k, tiles)
            row_copy(other).start()
            cell_copy(other).start()
            return carry

        lax.fori_loop(1 if b == faces else 0, tiles, send, 0)

    own_rows = pltpu.make_async_copy(rows_out.at[me], rows_in.at[me], own_sem.at[0])
    own_cells = pltpu.make_async_copy(cells_out.at[me], cells_in.at[me], own_sem.at[1])
    own_rows.start()
    own_cells.start()

    fill_taps(taps, wide_taps)
    wait_received(copies[:2])
    fill_columns(d, pad, rows, cols, hw, he)

    def step(i, carry):
        start = i * STEP
        for offset, piece in conv_rows(pad, wide_taps, bias, d, start, cols):
            at = pl.multiple_of((start + offset) * cols, d * cols)
            held[pl.ds(at, d * cols)] = jax.nn.gelu(piece, approximate=True).reshape(d * cols, channels)
        return carry

    steps = rows // STEP
    lax.fori_loop(1, steps - 1, step, 0, unroll=2)
    wait_received(copies[2:])
    for cond, copy in own:
        guarded(cond, copy.wait)
    fill_ends(faces, tiles, d, pad, rows, cols, north, south, corners, polar, link, turn)
    step(0, 0)
    step(steps - 1, 0)
    store = pltpu.make_async_copy(held, first, own_sem.at[4])
    store.start()
    wait_sent(copies)
    own_rows.wait()
    own_cells.wait()
    lax.fori_loop(1, count, finish, 0)
    store.wait()


def inject_kernel(d_next, cells, first, values, weight, mixed, pw_out, pe_out, total, encoded, sem):
    rows, cols, channels = mixed.shape
    sources, slots, features = values.shape
    cell_total = rows * cols
    load = pltpu.make_async_copy(first, total.at[pl.ds(0, cell_total)], sem)
    load.start()
    encoded[...] = jnp.dot(
        values[...].reshape(sources * slots, features), weight[...], preferred_element_type=jnp.float32
    )
    total[cell_total:] = jnp.zeros((total.shape[0] - cell_total, channels), jnp.float32)
    load.wait()
    group = GROUP

    def add_group(i, carry):
        source, at = i // (slots // group), lax.rem(i, slots // group) * group
        marked = [cells[source, at + j] for j in range(group)]

        @pl.when(marked[0] < cell_total)
        def _():
            any_repeat = functools.reduce(lambda x, y: x | y, marked) & REPEAT
            places = [m & (REPEAT - 1) for m in marked]
            chunk = encoded[pl.ds(pl.multiple_of(i * group, group), group)]

            @pl.when(any_repeat == 0)
            def _():
                sums = [total[pl.ds(places[j], 1)] + chunk[j : j + 1] for j in range(group)]
                for j in range(group):
                    total[pl.ds(places[j], 1)] = sums[j]

            @pl.when(any_repeat != 0)
            def _():
                for j in range(group):
                    total[pl.ds(places[j], 1)] += chunk[j : j + 1]

        return carry

    lax.fori_loop(0, sources * slots // group, add_group, 0)

    def step(i, carry):
        at = pl.multiple_of(i * STEP * cols, STEP * cols)
        here = total[pl.ds(at, STEP * cols)].reshape(STEP, cols, channels)
        mixed[pl.ds(i * STEP, STEP)] = here.astype(jnp.bfloat16)
        return carry

    lax.fori_loop(0, rows // STEP, step, 0)
    pw_out[...] = pack_columns(mixed[:, :EDGE].astype(jnp.float32), d_next, False)
    pe_out[...] = pack_columns(mixed[:, cols - EDGE :].astype(jnp.float32), d_next, True)


def second_kernel(
    faces, tiles, d, link, turn, taps, bias, grid, pw, pe, fields,
    out,
    pad, wide_taps, held, hw, he, north, south, corners, polar, send_sem, recv_sem, own_sem,
):
    rows, cols, channels = grid.shape
    s, t = lax.axis_index("face"), lax.axis_index("tile")
    barrier = pltpu.get_barrier_semaphore()

    def greet(to):
        pl.semaphore_signal(barrier, inc=1, device_id=to, device_id_type=MESH)

    east, west = lax.rem(s + 1, faces), lax.rem(s + faces - 1, faces)
    greet((east, t))
    greet((west, t))

    @pl.when(t > 0)
    def _():
        for f in (east, s, west):
            greet((f, t - 1))

    @pl.when(t < tiles - 1)
    def _():
        for f in (east, s, west):
            greet((f, t + 1))

    polar_end = (t == 0) | (t == tiles - 1)

    @pl.when(polar_end)
    def _():
        for k in range(2, faces - 1):
            greet((lax.rem(s + k, faces), t))

    own = own_polar(grid, polar, d, tiles, own_sem.at[0])
    for cond, copy in own:
        guarded(cond, copy.start)
    load = pltpu.make_async_copy(grid, pad.at[pl.ds(d, rows), pl.ds(0, cols)], own_sem.at[1])
    load.start()
    load_fields = pltpu.make_async_copy(fields, held, own_sem.at[2])
    load_fields.start()

    @pl.when(polar_end)
    def _():
        pl.semaphore_wait(barrier, 5 + faces - 3)

    @pl.when(jnp.logical_not(polar_end))
    def _():
        pl.semaphore_wait(barrier, 8)

    copies = start_halo(
        halo_sends(faces, tiles, d, grid, pw, pe, hw, he, north, south, corners, polar), send_sem, recv_sem
    )
    fill_taps(taps, wide_taps)
    load.wait()
    load_fields.wait()
    wait_received(copies[:2])
    fill_columns(d, pad, rows, cols, hw, he)

    def step(i, carry):
        start = i * STEP
        for offset, piece in conv_rows(pad, wide_taps, bias, d, start, cols):
            here = held[pl.ds(start + offset, d)].astype(jnp.float32)
            out[pl.ds(start + offset, d)] = (
                here + jax.nn.gelu(piece, approximate=True)
            ).astype(jnp.bfloat16)
        return carry

    steps = rows // STEP
    lax.fori_loop(1, steps - 1, step, 0, unroll=2)
    wait_received(copies[2:])
    for cond, copy in own:
        guarded(cond, copy.wait)
    fill_ends(faces, tiles, d, pad, rows, cols, north, south, corners, polar, link, turn)
    step(0, 0)
    step(steps - 1, 0)
    wait_sent(copies)


def local(
    fields, first_kernel_taps, first_conv_bias, second_kernel_taps, second_conv_bias,
    obs_weight, obs_values, obs_owner, obs_cells, polar_neighbor_sector, polar_link_reversal,
):
    faces, tiles = lax.axis_size("face"), lax.axis_size("tile")
    rows, cols, channels = fields.shape
    obs_rows, features = obs_values.shape
    dest_count = faces * tiles
    slots = 2 * obs_rows // dest_count
    cell_total = rows * cols
    bf16, f32, i32 = jnp.bfloat16, jnp.float32, jnp.int32
    shape = jax.ShapeDtypeStruct
    vmem = pl.BlockSpec(memory_space=pltpu.VMEM)
    smem = pl.BlockSpec(memory_space=pltpu.SMEM)
    anywhere = pl.BlockSpec(memory_space=pl.ANY)
    dma = pltpu.SemaphoreType.DMA
    d1, d2 = FIRST_DILATION, SECOND_DILATION
    halo_copies = 8 + 2 * (faces - 1)
    link, turn = polar_neighbor_sector.T, polar_link_reversal.T

    def packed_dims(d):
        return (rows * d // EDGE, EDGE, channels)

    def conv_scratch(d):
        return [
            pltpu.VMEM((rows + 2 * d, cols + EDGE, channels), bf16),
            pltpu.VMEM((4 * channels, 6 * channels), bf16),
        ]

    def halo_scratch(d):
        return [
            pltpu.VMEM(packed_dims(d), bf16), pltpu.VMEM(packed_dims(d), bf16),
            pltpu.VMEM((d, cols, channels), bf16), pltpu.VMEM((d, cols, channels), bf16),
            pltpu.VMEM((4, d, EDGE, channels), bf16), pltpu.VMEM((faces, d, cols, channels), bf16),
        ]

    first, recv_rows, recv_cells = pl.pallas_call(
        functools.partial(first_kernel, faces, tiles, d1, slots),
        out_shape=[
            shape((cell_total, channels), f32),
            shape((dest_count, slots, features), bf16),
            shape((dest_count, 1, LANES), i32),
        ],
        in_specs=[smem] * 2 + [vmem] * 5 + [anywhere],
        out_specs=[anywhere] * 3,
        scratch_shapes=conv_scratch(d1) + [
            pltpu.VMEM((cell_total, channels), f32),
            pltpu.VMEM((dest_count, slots, features), bf16),
            pltpu.VMEM((dest_count, 1, LANES), i32),
            pltpu.VMEM(packed_dims(d1), bf16), pltpu.VMEM(packed_dims(d1), bf16),
        ] + halo_scratch(d1) + [
            dma((halo_copies,)), dma((halo_copies,)), dma((dest_count,)), dma((dest_count,)),
            dma((dest_count,)), dma((dest_count,)), dma((5,)),
        ],
        compiler_params=pltpu.CompilerParams(
            collective_id=0, has_side_effects=True, vmem_limit_bytes=VMEM_LIMIT
        ),
        name="first_conv_and_exchange",
    )(
        link, turn, obs_owner.reshape(1, obs_rows), obs_cells.reshape(1, obs_rows), obs_values,
        first_kernel_taps, first_conv_bias.reshape(1, channels), fields,
    )

    mixed, pw, pe = pl.pallas_call(
        functools.partial(inject_kernel, d2),
        out_shape=[
            shape((rows, cols, channels), bf16), shape(packed_dims(d2), bf16), shape(packed_dims(d2), bf16)
        ],
        in_specs=[smem, anywhere, vmem, vmem],
        out_specs=[vmem] * 3,
        scratch_shapes=[
            pltpu.VMEM((cell_total + 8, channels), f32),
            pltpu.VMEM((dest_count * slots, channels), f32),
            dma,
        ],
        compiler_params=pltpu.CompilerParams(vmem_limit_bytes=VMEM_LIMIT),
        name="inject",
    )(recv_cells.reshape(dest_count, LANES), first, recv_rows, obs_weight)

    return pl.pallas_call(
        functools.partial(second_kernel, faces, tiles, d2),
        out_shape=shape((rows, cols, channels), bf16),
        in_specs=[smem] * 2 + [vmem] * 2 + [anywhere] * 4,
        out_specs=vmem,
        scratch_shapes=conv_scratch(d2) + [pltpu.VMEM((rows, cols, channels), bf16)]
        + halo_scratch(d2) + [dma((halo_copies,)), dma((halo_copies,)), dma((3,))],
        compiler_params=pltpu.CompilerParams(
            collective_id=1, has_side_effects=True, vmem_limit_bytes=VMEM_LIMIT
        ),
        name="second_conv_and_exchange",
    )(
        link, turn, second_kernel_taps, second_conv_bias.reshape(1, channels), mixed, pw, pe, fields
    )


def solution(mesh):
    in_specs = (
        P("tile", "face", None), P(), P(), P(), P(), P(),
        P(("face", "tile"), None), P(("face", "tile"), None), P(("face", "tile")), P(), P(),
    )
    return jax.shard_map(
        local, mesh=mesh, in_specs=in_specs, out_specs=P("tile", "face", None), check_vma=False
    )
```

```python
import functools

import jax
import jax.numpy as jnp
from jax import lax
from jax.experimental import pallas as pl
from jax.experimental.pallas import tpu as pltpu
from jax.sharding import PartitionSpec as P

FIRST_DILATION = 2
SECOND_DILATION = 4
MESH = pl.DeviceIdType.MESH
LANES = 128
EDGE = 16
STEP = 8
GROUP = 16
REPEAT = 1 << 14
VMEM_LIMIT = 56 * 1024 * 1024


def pack_columns(tile, d, east):
    rows, _, ch = tile.shape
    per = 8 // d
    half = tile[:, 8:] if east else tile[:, :8]
    grouped = half.reshape(rows // per, per, 8, ch)
    sub = lax.broadcasted_iota(jnp.int32, (rows // per, 8, ch), 1)
    out = None
    for j in range(per):
        shift = (j * d - (8 - d if east else 0)) % 8
        part = grouped[:, j]
        if shift:
            part = pltpu.roll(part, shift, 1)
        out = part if out is None else jnp.where(sub >= j * d, part, out)
    return out.reshape(rows // (2 * per), EDGE, ch).astype(jnp.bfloat16)


def unpack_columns(packed, d, west):
    count, _, ch = packed.shape
    per = 8 // d
    pieces = packed.astype(jnp.float32).reshape(2 * count, 8, ch)
    parts = []
    for j in range(per):
        shift = ((8 - d if west else 0) - j * d) % 8
        parts.append(pltpu.roll(pieces, shift, 1) if shift else pieces)
    return jnp.stack(parts, axis=1).reshape(2 * count * per, 8, ch)


def join_edge(east_tile, west_tile):
    east = east_tile.astype(jnp.float32)
    west = west_tile.astype(jnp.float32)
    axis = east.ndim - 2
    return jnp.concatenate(
        [lax.slice_in_dim(east, 0, 8, axis=axis), lax.slice_in_dim(west, 8, 16, axis=axis)], axis=axis
    ).astype(jnp.bfloat16)


def rank_observations(dest_count, slots, owner_ref, cells_ref):
    obs = owner_ref.shape[1]
    owner = owner_ref[...]
    dests = lax.broadcasted_iota(jnp.int32, (dest_count, obs), 0)
    onehot = jnp.where(dests == owner, 1.0, 0.0)
    before = (
        lax.broadcasted_iota(jnp.int32, (obs, obs), 0) < lax.broadcasted_iota(jnp.int32, (obs, obs), 1)
    )
    ranks = jnp.dot(
        onehot.astype(jnp.bfloat16),
        jnp.where(before, 1.0, 0.0).astype(jnp.bfloat16),
        preferred_element_type=jnp.float32,
    )
    rank = jnp.sum(ranks * onehot, axis=0, keepdims=True).astype(jnp.int32)
    target = owner * slots + rank
    cells = cells_ref[...]
    kind = lax.broadcasted_iota(jnp.int32, (8, obs), 0)
    codes = jnp.where(kind == 0, cells >> 7, jnp.where(kind == 1, cells & 127, 1))
    codes = codes.astype(jnp.float32).astype(jnp.bfloat16)
    return target, codes


def pack_block(block, slots, cell_total, face, target, codes, values, rows_out, cells_out):
    obs = target.shape[1]
    first = face * (block // slots)
    wanted = face * block + lax.broadcasted_iota(jnp.int32, (block, obs), 0)
    match = jnp.where(wanted == target, 1.0, 0.0).astype(jnp.bfloat16)
    rows = jnp.dot(match, values[...], preferred_element_type=jnp.float32).astype(jnp.bfloat16)
    rows_out[pl.ds(first, block // slots)] = rows.reshape(block // slots, slots, rows.shape[-1])
    got = lax.dot_general(codes, match, (((1,), (1,)), ((), ())), preferred_element_type=jnp.float32)
    found = (got[0:1] * LANES + got[1:2]).astype(jnp.int32)
    found = jnp.broadcast_to(jnp.where(got[2:3] > 0.5, found, cell_total), (8, block))
    place = lax.broadcasted_iota(jnp.int32, (8, block), 1) & (GROUP - 1)
    repeats = jnp.zeros((8, block), jnp.int32)
    for k in range(1, GROUP):
        same = (found == pltpu.roll(found, k, 1)) & (place >= k) & (found < cell_total)
        repeats = jnp.where(same, REPEAT, repeats)
    found = found + repeats
    for j in range(block // slots):
        cells_out[first + j, :, :slots] = found[:1, j * slots : (j + 1) * slots]


def halo_sends(faces, tiles, d, grid, pw, pe, hw, he, north, south, corners, polar):
    s, t = lax.axis_index("face"), lax.axis_index("tile")
    rows, cols = grid.shape[0], grid.shape[1]
    east, west = lax.rem(s + 1, faces), lax.rem(s + faces - 1, faces)
    last, first = pl.ds(rows - d, d), pl.ds(0, d)
    right, left = pl.ds(cols - EDGE, EDGE), pl.ds(0, EDGE)
    not_top, not_low = t > 0, t < tiles - 1
    up, down = t - 1, t + 1
    plan = [
        (None, None, pe, hw, (east, t)),
        (None, None, pw, he, (west, t)),
        (not_low, not_top, grid.at[last], north, (s, down)),
        (not_top, not_low, grid.at[first], south, (s, up)),
        (not_low, not_top, grid.at[last, right], corners.at[0], (east, down)),
        (not_low, not_top, grid.at[last, left], corners.at[1], (west, down)),
        (not_top, not_low, grid.at[first, right], corners.at[2], (east, up)),
        (not_top, not_low, grid.at[first, left], corners.at[3], (west, up)),
    ]
    for k in range(1, faces):
        to = (lax.rem(s + k, faces), t)
        plan.append((t == 0, t == 0, grid.at[first], polar.at[s], to))
    for k in range(1, faces):
        to = (lax.rem(s + k, faces), t)
        plan.append((t == tiles - 1, t == tiles - 1, grid.at[last], polar.at[s], to))
    return plan


def guarded(cond, action):
    if cond is None:
        action()
    else:
        pl.when(cond)(action)


def start_halo(plan, send_sem, recv_sem):
    copies = []
    for i, (sends, receives, src, dst, to) in enumerate(plan):
        copy = pltpu.make_async_remote_copy(
            src_ref=src, dst_ref=dst, send_sem=send_sem.at[i], recv_sem=recv_sem.at[i],
            device_id=to, device_id_type=MESH,
        )
        guarded(sends, copy.start)
        copies.append((sends, receives, copy))
    return copies


def wait_received(copies):
    for _, receives, copy in copies:
        guarded(receives, copy.wait_recv)


def wait_sent(copies):
    for sends, _, copy in copies:
        guarded(sends, copy.wait_send)


def own_polar(grid, polar, d, tiles, sem):
    s, t = lax.axis_index("face"), lax.axis_index("tile")
    top = pltpu.make_async_copy(grid.at[pl.ds(0, d)], polar.at[s], sem)
    low = pltpu.make_async_copy(grid.at[pl.ds(grid.shape[0] - d, d)], polar.at[s], sem)
    return [(t == 0, top), (t == tiles - 1, low)]


def fill_columns(d, pad, rows, cols, hw, he):
    pad[d : d + rows, cols:] = jnp.concatenate(
        [unpack_columns(he[...], d, False), unpack_columns(hw[...], d, True)], axis=1
    ).astype(jnp.bfloat16)


def fill_ends(faces, tiles, d, pad, rows, cols, north, south, corners, polar, link, turn):
    s, t = lax.axis_index("face"), lax.axis_index("tile")
    wide = cols + EDGE

    def from_pole(base, column):
        p = link[column, s]
        east, west = lax.rem(p + 1, faces), lax.rem(p + faces - 1, faces)
        here = lax.broadcasted_iota(jnp.int32, (wide, wide), 0)
        there = lax.broadcasted_iota(jnp.int32, (wide, wide), 1)
        mirrored = jnp.where(here < cols, cols - 1 - here, wide + cols - 1 - here)
        source = jnp.where(turn[column, s] == 1, mirrored, here)
        move = jnp.where(there == source, 1.0, 0.0).astype(jnp.bfloat16)
        for i in range(d):
            k = d - 1 - i
            edge = join_edge(polar[east, k, :EDGE], polar[west, k, cols - EDGE :])
            line = jnp.concatenate([polar[p, k], edge], axis=0)
            pad[base + i] = jnp.dot(move, line, preferred_element_type=jnp.float32).astype(jnp.bfloat16)

    @pl.when(t == 0)
    def _():
        from_pole(0, 0)

    @pl.when(t > 0)
    def _():
        pad[:d, :cols] = north[...]
        pad[:d, cols:] = join_edge(corners[1], corners[0])

    @pl.when(t == tiles - 1)
    def _():
        from_pole(d + rows, 1)

    @pl.when(t < tiles - 1)
    def _():
        pad[d + rows :, :cols] = south[...]
        pad[d + rows :, cols:] = join_edge(corners[3], corners[2])


def fill_taps(taps, wide_taps):
    channels, features = taps.shape[1], taps.shape[2]
    for k in range(4):
        for e in range(3):
            for j in range(2):
                piece = (
                    taps[3 * (k - j) + e] if 0 <= k - j <= 2 else jnp.zeros((channels, features), jnp.bfloat16)
                )
                at = (2 * e + j) * features
                wide_taps[k * channels : (k + 1) * channels, at : at + features] = piece


def conv_rows(pad, wide_taps, bias, d, start, cols):
    wide = cols + EDGE
    features = bias.shape[-1]
    count = STEP // (2 * d)
    lines = []
    for k in range(4):
        blocks = [pad[pl.ds(start + m * 2 * d + k * d, d)] for m in range(count)]
        lines.append(jnp.concatenate(blocks, axis=0).reshape(count * d * wide, pad.shape[-1]))
    product = jnp.dot(
        jnp.concatenate(lines, axis=1), wide_taps[...], preferred_element_type=jnp.float32
    ).reshape(count * d, wide, 6 * features)
    halves = []
    for j in range(2):
        low, middle, high = (
            product[:, :, (2 * e + j) * features : (2 * e + j + 1) * features] for e in range(3)
        )
        total = pltpu.roll(low, d, 1) + middle + pltpu.roll(high, wide - d, 1)
        halves.append(total[:, :cols] + bias[...].reshape(1, 1, features))
    return [(m * 2 * d + j * d, halves[j][m * d : (m + 1) * d]) for m in range(count) for j in range(2)]


def fill_edge_taps(taps, edge_taps):
    channels, features = taps.shape[1], taps.shape[2]
    for a in range(3):
        for i, e in enumerate((0, 2)):
            edge_taps[a * channels : (a + 1) * channels, i * features : (i + 1) * features] = taps[3 * a + e]


def conv_inner(pad, wide_taps, bias, d, start, cols, edges):
    features = bias.shape[-1]
    count = STEP // (2 * d)
    lines = []
    for k in range(4):
        blocks = [pad[pl.ds(start + m * 2 * d + k * d, d), :cols] for m in range(count)]
        lines.append(jnp.concatenate(blocks, axis=0).reshape(count * d * cols, pad.shape[-1]))
    product = jnp.dot(
        jnp.concatenate(lines, axis=1), wide_taps[...], preferred_element_type=jnp.float32
    ).reshape(count * d, cols, 6 * features)
    shift = bias[...].reshape(1, 1, features)
    sub = lax.broadcasted_iota(jnp.int32, (count * d, 8, features), 1)
    pieces = []
    for j in range(2):
        low, middle, high = (
            product[:, :, (2 * e + j) * features : (2 * e + j + 1) * features] for e in range(3)
        )
        low = pltpu.roll(low, d, 1)
        high = pltpu.roll(high, cols - d, 1)
        middle = middle + shift
        left = middle[:, :8] + high[:, :8] + jnp.where(sub < d, 0.0, low[:, :8])
        right = middle[:, cols - 8 :] + low[:, cols - 8 :] + jnp.where(sub >= 8 - d, 0.0, high[:, cols - 8 :])
        total = low + middle + high
        for m in range(count):
            offset = m * 2 * d + j * d
            edges[0, pl.ds(start + offset, d)] = left[m * d : (m + 1) * d]
            edges[1, pl.ds(start + offset, d)] = right[m * d : (m + 1) * d]
            pieces.append((offset, total[m * d : (m + 1) * d]))
    return pieces


def finish_edges(pad, edge_taps, d, start, size, cols, edges, held, out):
    features = edges.shape[-1]
    lines = [
        pad[pl.ds(start + a * d, size), cols:].reshape(size * EDGE, pad.shape[-1]) for a in range(3)
    ]
    product = jnp.dot(
        jnp.concatenate(lines, axis=1), edge_taps[...], preferred_element_type=jnp.float32
    ).reshape(size, EDGE, 2 * features)
    sub = lax.broadcasted_iota(jnp.int32, (size, 8, features), 1)
    here = pl.ds(start, size)
    from_west = pltpu.roll(product[:, 8:, :features], d, 1)
    left = edges[0, here] + jnp.where(sub < d, from_west, 0.0)
    from_east = pltpu.roll(product[:, :8, features:], 8 - d, 1)
    right = edges[1, here] + jnp.where(sub >= 8 - d, from_east, 0.0)
    kept = out[here, :EDGE].astype(jnp.float32)[:, 8:]
    fresh = held[here, :EDGE].astype(jnp.float32)[:, :8] + jax.nn.gelu(left, approximate=True)
    out[here, :EDGE] = jnp.concatenate([fresh, kept], axis=1).astype(jnp.bfloat16)
    kept = out[here, cols - EDGE :].astype(jnp.float32)[:, :8]
    fresh = held[here, cols - EDGE :].astype(jnp.float32)[:, 8:] + jax.nn.gelu(right, approximate=True)
    out[here, cols - EDGE :] = jnp.concatenate([kept, fresh], axis=1).astype(jnp.bfloat16)


def first_kernel(
    faces, tiles, d, slots,
    link, turn, owner, cells, values, taps, bias, grid,
    first, rows_in, cells_in,
    pad, wide_taps, held, rows_out, cells_out, pw, pe, hw, he, north, south, corners, polar,
    send_sem, recv_sem, row_send, row_recv, cell_send, cell_recv, own_sem,
):
    rows, cols, channels = grid.shape
    cell_total = rows * cols
    count = faces * tiles
    me = lax.axis_index("face") * tiles + lax.axis_index("tile")
    barrier = pltpu.get_barrier_semaphore()
    load = pltpu.make_async_copy(grid, pad.at[pl.ds(d, rows), pl.ds(0, cols)], own_sem.at[3])
    load.start()

    def device(k):
        other = lax.rem(me + k, count)
        return other, (other // tiles, lax.rem(other, tiles))

    def greet(k, carry):
        _, to = device(k)
        pl.semaphore_signal(barrier, inc=1, device_id=to, device_id_type=MESH)
        return carry

    lax.fori_loop(1, count, greet, 0)
    own = own_polar(grid, polar, d, tiles, own_sem.at[2])
    for cond, copy in own:
        guarded(cond, copy.start)
    cells_out[...] = jnp.full(cells_out.shape, cell_total, jnp.int32)
    target, codes = rank_observations(count, slots, owner, cells)
    load.wait()
    pw[...] = pack_columns(pad[d : d + rows, :EDGE].astype(jnp.float32), d, False)
    pe[...] = pack_columns(pad[d : d + rows, cols - EDGE : cols].astype(jnp.float32), d, True)
    pl.semaphore_wait(barrier, count - 1)
    copies = start_halo(
        halo_sends(faces, tiles, d, grid, pw, pe, hw, he, north, south, corners, polar), send_sem, recv_sem
    )

    def row_copy(other):
        to = (other // tiles, lax.rem(other, tiles))
        return pltpu.make_async_remote_copy(
            src_ref=rows_out.at[other], dst_ref=rows_in.at[me],
            send_sem=row_send.at[lax.rem(other + count - me, count)],
            recv_sem=row_recv.at[lax.rem(other + count - me, count)],
            device_id=to, device_id_type=MESH,
        )

    def cell_copy(other):
        to = (other // tiles, lax.rem(other, tiles))
        return pltpu.make_async_remote_copy(
            src_ref=cells_out.at[other], dst_ref=cells_in.at[me],
            send_sem=cell_send.at[lax.rem(other + count - me, count)],
            recv_sem=cell_recv.at[lax.rem(other + count - me, count)],
            device_id=to, device_id_type=MESH,
        )

    def finish(k, carry):
        other = lax.rem(me + k, count)
        row_copy(other).wait()
        cell_copy(other).wait()
        return carry

    s, t = lax.axis_index("face"), lax.axis_index("tile")
    for b in range(1, faces + 1):
        face = lax.rem(s + b, faces)
        pack_block(tiles * slots, slots, cell_total, face, target, codes, values, rows_out, cells_out)

        def send(k, carry, face=face):
            other = face * tiles + lax.rem(t + k, tiles)
            row_copy(other).start()
            cell_copy(other).start()
            return carry

        lax.fori_loop(1 if b == faces else 0, tiles, send, 0)

    own_rows = pltpu.make_async_copy(rows_out.at[me], rows_in.at[me], own_sem.at[0])
    own_cells = pltpu.make_async_copy(cells_out.at[me], cells_in.at[me], own_sem.at[1])
    own_rows.start()
    own_cells.start()

    fill_taps(taps, wide_taps)
    wait_received(copies[:2])
    fill_columns(d, pad, rows, cols, hw, he)

    def step(i, carry):
        start = i * STEP
        for offset, piece in conv_rows(pad, wide_taps, bias, d, start, cols):
            at = pl.multiple_of((start + offset) * cols, d * cols)
            held[pl.ds(at, d * cols)] = jax.nn.gelu(piece, approximate=True).reshape(d * cols, channels)
        return carry

    steps = rows // STEP
    lax.fori_loop(1, steps - 1, step, 0, unroll=2)
    stores = []
    for i, (begin, size) in enumerate([(STEP, rows - 2 * STEP), (0, STEP), (rows - STEP, STEP)]):
        part = pl.ds(begin * cols, size * cols)
        stores.append(pltpu.make_async_copy(held.at[part], first.at[part], own_sem.at[4 + i]))
    stores[0].start()
    wait_received(copies[2:])
    for cond, copy in own:
        guarded(cond, copy.wait)
    fill_ends(faces, tiles, d, pad, rows, cols, north, south, corners, polar, link, turn)
    step(0, 0)
    step(steps - 1, 0)
    stores[1].start()
    stores[2].start()
    wait_sent(copies)
    own_rows.wait()
    own_cells.wait()
    lax.fori_loop(1, count, finish, 0)
    for store in stores:
        store.wait()


def inject_kernel(d_next, cells, first, values, weight, mixed, pw_out, pe_out, total, encoded, sem):
    rows, cols, channels = mixed.shape
    sources, slots, features = values.shape
    cell_total = rows * cols
    load = pltpu.make_async_copy(first, total.at[pl.ds(0, cell_total)], sem)
    load.start()
    encoded[...] = jnp.dot(
        values[...].reshape(sources * slots, features), weight[...], preferred_element_type=jnp.float32
    )
    total[cell_total:] = jnp.zeros((total.shape[0] - cell_total, channels), jnp.float32)
    load.wait()
    group = GROUP

    def add_group(i, carry):
        source, at = i // (slots // group), lax.rem(i, slots // group) * group
        marked = [cells[source, at + j] for j in range(group)]

        @pl.when(marked[0] < cell_total)
        def _():
            any_repeat = functools.reduce(lambda x, y: x | y, marked) & REPEAT
            places = [m & (REPEAT - 1) for m in marked]

            def row(j):
                return encoded[pl.ds(i * group + j, 1)]

            @pl.when(any_repeat == 0)
            def _():
                sums = [total[pl.ds(places[j], 1)] + row(j) for j in range(group)]
                for j in range(group):
                    total[pl.ds(places[j], 1)] = sums[j]

            @pl.when(any_repeat != 0)
            def _():
                for j in range(group):
                    total[pl.ds(places[j], 1)] += row(j)

        return carry

    lax.fori_loop(0, sources * slots // group, add_group, 0)

    def step(i, carry):
        at = pl.multiple_of(i * STEP * cols, STEP * cols)
        here = total[pl.ds(at, STEP * cols)].reshape(STEP, cols, channels)
        mixed[pl.ds(i * STEP, STEP)] = here.astype(jnp.bfloat16)
        return carry

    lax.fori_loop(0, rows // STEP, step, 0)
    pw_out[...] = pack_columns(mixed[:, :EDGE].astype(jnp.float32), d_next, False)
    pe_out[...] = pack_columns(mixed[:, cols - EDGE :].astype(jnp.float32), d_next, True)


def second_kernel(
    faces, tiles, d, link, turn, taps, bias, grid, pw, pe, fields,
    out,
    pad, wide_taps, held, edge_taps, edges, hw, he, north, south, corners, polar,
    send_sem, recv_sem, own_sem,
):
    rows, cols, channels = grid.shape
    s, t = lax.axis_index("face"), lax.axis_index("tile")
    barrier = pltpu.get_barrier_semaphore()

    def greet(to):
        pl.semaphore_signal(barrier, inc=1, device_id=to, device_id_type=MESH)

    east, west = lax.rem(s + 1, faces), lax.rem(s + faces - 1, faces)
    greet((east, t))
    greet((west, t))

    @pl.when(t > 0)
    def _():
        for f in (east, s, west):
            greet((f, t - 1))

    @pl.when(t < tiles - 1)
    def _():
        for f in (east, s, west):
            greet((f, t + 1))

    polar_end = (t == 0) | (t == tiles - 1)

    @pl.when(polar_end)
    def _():
        for k in range(2, faces - 1):
            greet((lax.rem(s + k, faces), t))

    own = own_polar(grid, polar, d, tiles, own_sem.at[0])
    for cond, copy in own:
        guarded(cond, copy.start)
    load = pltpu.make_async_copy(grid, pad.at[pl.ds(d, rows), pl.ds(0, cols)], own_sem.at[1])
    load.start()
    load_fields = pltpu.make_async_copy(fields, held, own_sem.at[2])
    load_fields.start()

    @pl.when(polar_end)
    def _():
        pl.semaphore_wait(barrier, 5 + faces - 3)

    @pl.when(jnp.logical_not(polar_end))
    def _():
        pl.semaphore_wait(barrier, 8)

    copies = start_halo(
        halo_sends(faces, tiles, d, grid, pw, pe, hw, he, north, south, corners, polar), send_sem, recv_sem
    )
    fill_taps(taps, wide_taps)
    fill_edge_taps(taps, edge_taps)
    load.wait()
    load_fields.wait()

    def write(start, pieces):
        for offset, piece in pieces:
            here = held[pl.ds(start + offset, d)].astype(jnp.float32)
            out[pl.ds(start + offset, d)] = (
                here + jax.nn.gelu(piece, approximate=True)
            ).astype(jnp.bfloat16)

    def inner(i, carry):
        write(i * STEP, conv_inner(pad, wide_taps, bias, d, i * STEP, cols, edges))
        return carry

    def finish(i, carry):
        finish_edges(pad, edge_taps, d, i * 2 * STEP + STEP, 2 * STEP, cols, edges, held, out)
        return carry

    steps = rows // STEP
    lax.fori_loop(1, steps - 1, inner, 0, unroll=2)
    wait_received(copies[:2])
    fill_columns(d, pad, rows, cols, hw, he)
    lax.fori_loop(0, (steps - 2) // 2, finish, 0)
    wait_received(copies[2:])
    for cond, copy in own:
        guarded(cond, copy.wait)
    fill_ends(faces, tiles, d, pad, rows, cols, north, south, corners, polar, link, turn)
    for start in (0, rows - STEP):
        write(start, conv_rows(pad, wide_taps, bias, d, start, cols))
    wait_sent(copies)


def local(
    fields, first_kernel_taps, first_conv_bias, second_kernel_taps, second_conv_bias,
    obs_weight, obs_values, obs_owner, obs_cells, polar_neighbor_sector, polar_link_reversal,
):
    faces, tiles = lax.axis_size("face"), lax.axis_size("tile")
    rows, cols, channels = fields.shape
    obs_rows, features = obs_values.shape
    dest_count = faces * tiles
    slots = 2 * obs_rows // dest_count
    cell_total = rows * cols
    bf16, f32, i32 = jnp.bfloat16, jnp.float32, jnp.int32
    shape = jax.ShapeDtypeStruct
    vmem = pl.BlockSpec(memory_space=pltpu.VMEM)
    smem = pl.BlockSpec(memory_space=pltpu.SMEM)
    anywhere = pl.BlockSpec(memory_space=pl.ANY)
    dma = pltpu.SemaphoreType.DMA
    d1, d2 = FIRST_DILATION, SECOND_DILATION
    halo_copies = 8 + 2 * (faces - 1)
    link, turn = polar_neighbor_sector.T, polar_link_reversal.T

    def packed_dims(d):
        return (rows * d // EDGE, EDGE, channels)

    def conv_scratch(d):
        return [
            pltpu.VMEM((rows + 2 * d, cols + EDGE, channels), bf16),
            pltpu.VMEM((4 * channels, 6 * channels), bf16),
        ]

    def halo_scratch(d):
        return [
            pltpu.VMEM(packed_dims(d), bf16), pltpu.VMEM(packed_dims(d), bf16),
            pltpu.VMEM((d, cols, channels), bf16), pltpu.VMEM((d, cols, channels), bf16),
            pltpu.VMEM((4, d, EDGE, channels), bf16), pltpu.VMEM((faces, d, cols, channels), bf16),
        ]

    first, recv_rows, recv_cells = pl.pallas_call(
        functools.partial(first_kernel, faces, tiles, d1, slots),
        out_shape=[
            shape((cell_total, channels), f32),
            shape((dest_count, slots, features), bf16),
            shape((dest_count, 1, LANES), i32),
        ],
        in_specs=[smem] * 2 + [vmem] * 5 + [anywhere],
        out_specs=[anywhere] * 3,
        scratch_shapes=conv_scratch(d1) + [
            pltpu.VMEM((cell_total, channels), f32),
            pltpu.VMEM((dest_count, slots, features), bf16),
            pltpu.VMEM((dest_count, 1, LANES), i32),
            pltpu.VMEM(packed_dims(d1), bf16), pltpu.VMEM(packed_dims(d1), bf16),
        ] + halo_scratch(d1) + [
            dma((halo_copies,)), dma((halo_copies,)), dma((dest_count,)), dma((dest_count,)),
            dma((dest_count,)), dma((dest_count,)), dma((7,)),
        ],
        compiler_params=pltpu.CompilerParams(
            collective_id=0, has_side_effects=True, vmem_limit_bytes=VMEM_LIMIT
        ),
        name="first_conv_and_exchange",
    )(
        link, turn, obs_owner.reshape(1, obs_rows), obs_cells.reshape(1, obs_rows), obs_values,
        first_kernel_taps, first_conv_bias.reshape(1, channels), fields,
    )

    mixed, pw, pe = pl.pallas_call(
        functools.partial(inject_kernel, d2),
        out_shape=[
            shape((rows, cols, channels), bf16), shape(packed_dims(d2), bf16), shape(packed_dims(d2), bf16)
        ],
        in_specs=[smem, anywhere, vmem, vmem],
        out_specs=[vmem] * 3,
        scratch_shapes=[
            pltpu.VMEM((cell_total + 8, channels), f32),
            pltpu.VMEM((dest_count * slots, channels), f32),
            dma,
        ],
        compiler_params=pltpu.CompilerParams(vmem_limit_bytes=VMEM_LIMIT),
        name="inject",
    )(recv_cells.reshape(dest_count, LANES), first, recv_rows, obs_weight)

    return pl.pallas_call(
        functools.partial(second_kernel, faces, tiles, d2),
        out_shape=shape((rows, cols, channels), bf16),
        in_specs=[smem] * 2 + [vmem] * 2 + [anywhere] * 4,
        out_specs=vmem,
        scratch_shapes=conv_scratch(d2) + [
            pltpu.VMEM((rows, cols, channels), bf16),
            pltpu.VMEM((3 * channels, 2 * channels), bf16),
            pltpu.VMEM((2, rows, 8, channels), f32),
        ] + halo_scratch(d2) + [dma((halo_copies,)), dma((halo_copies,)), dma((3,))],
        compiler_params=pltpu.CompilerParams(
            collective_id=1, has_side_effects=True, vmem_limit_bytes=VMEM_LIMIT
        ),
        name="second_conv_and_exchange",
    )(
        link, turn, second_kernel_taps, second_conv_bias.reshape(1, channels), mixed, pw, pe, fields
    )


def solution(mesh):
    in_specs = (
        P("tile", "face", None), P(), P(), P(), P(), P(),
        P(("face", "tile"), None), P(("face", "tile"), None), P(("face", "tile")), P(), P(),
    )
    return jax.shard_map(
        local, mesh=mesh, in_specs=in_specs, out_specs=P("tile", "face", None), check_vma=False
    )
```

```python
import functools

import jax
import jax.numpy as jnp
from jax import lax
from jax.experimental import pallas as pl
from jax.experimental.pallas import tpu as pltpu
from jax.sharding import PartitionSpec as P

FIRST_DILATION = 2
SECOND_DILATION = 4
MESH = pl.DeviceIdType.MESH
LANES = 128
EDGE = 16
STEP = 8
GROUP = 16
REPEAT = 1 << 14
CHUNKS = 4
VMEM_LIMIT = 56 * 1024 * 1024


def pack_columns(tile, d, east):
    rows, _, ch = tile.shape
    per = 8 // d
    half = tile[:, 8:] if east else tile[:, :8]
    grouped = half.reshape(rows // per, per, 8, ch)
    sub = lax.broadcasted_iota(jnp.int32, (rows // per, 8, ch), 1)
    out = None
    for j in range(per):
        shift = (j * d - (8 - d if east else 0)) % 8
        part = grouped[:, j]
        if shift:
            part = pltpu.roll(part, shift, 1)
        out = part if out is None else jnp.where(sub >= j * d, part, out)
    return out.reshape(rows // (2 * per), EDGE, ch).astype(jnp.bfloat16)


def unpack_columns(packed, d, west):
    count, _, ch = packed.shape
    per = 8 // d
    pieces = packed.astype(jnp.float32).reshape(2 * count, 8, ch)
    parts = []
    for j in range(per):
        shift = ((8 - d if west else 0) - j * d) % 8
        parts.append(pltpu.roll(pieces, shift, 1) if shift else pieces)
    return jnp.stack(parts, axis=1).reshape(2 * count * per, 8, ch)


def join_edge(east_tile, west_tile):
    east = east_tile.astype(jnp.float32)
    west = west_tile.astype(jnp.float32)
    axis = east.ndim - 2
    return jnp.concatenate(
        [lax.slice_in_dim(east, 0, 8, axis=axis), lax.slice_in_dim(west, 8, 16, axis=axis)], axis=axis
    ).astype(jnp.bfloat16)


def rank_observations(dest_count, slots, owner_ref, cells_ref):
    obs = owner_ref.shape[1]
    owner = owner_ref[...]
    dests = lax.broadcasted_iota(jnp.int32, (dest_count, obs), 0)
    onehot = jnp.where(dests == owner, 1.0, 0.0)
    before = (
        lax.broadcasted_iota(jnp.int32, (obs, obs), 0) < lax.broadcasted_iota(jnp.int32, (obs, obs), 1)
    )
    ranks = jnp.dot(
        onehot.astype(jnp.bfloat16),
        jnp.where(before, 1.0, 0.0).astype(jnp.bfloat16),
        preferred_element_type=jnp.float32,
    )
    rank = jnp.sum(ranks * onehot, axis=0, keepdims=True).astype(jnp.int32)
    target = owner * slots + rank
    cells = cells_ref[...]
    kind = lax.broadcasted_iota(jnp.int32, (8, obs), 0)
    codes = jnp.where(kind == 0, cells >> 7, jnp.where(kind == 1, cells & 127, 1))
    codes = codes.astype(jnp.float32).astype(jnp.bfloat16)
    return target, codes


def pack_block(block, slots, cell_total, face, target, codes, values, rows_out, cells_out):
    obs = target.shape[1]
    first = face * (block // slots)
    wanted = face * block + lax.broadcasted_iota(jnp.int32, (block, obs), 0)
    match = jnp.where(wanted == target, 1.0, 0.0).astype(jnp.bfloat16)
    rows = jnp.dot(match, values[...], preferred_element_type=jnp.float32).astype(jnp.bfloat16)
    rows_out[pl.ds(first, block // slots)] = rows.reshape(block // slots, slots, rows.shape[-1])
    got = lax.dot_general(codes, match, (((1,), (1,)), ((), ())), preferred_element_type=jnp.float32)
    found = (got[0:1] * LANES + got[1:2]).astype(jnp.int32)
    found = jnp.broadcast_to(jnp.where(got[2:3] > 0.5, found, cell_total), (8, block))
    place = lax.broadcasted_iota(jnp.int32, (8, block), 1) & (GROUP - 1)
    repeats = jnp.zeros((8, block), jnp.int32)
    for k in range(1, GROUP):
        same = (found == pltpu.roll(found, k, 1)) & (place >= k) & (found < cell_total)
        repeats = jnp.where(same, REPEAT, repeats)
    found = found + repeats
    for j in range(block // slots):
        cells_out[first + j, :, :slots] = found[:1, j * slots : (j + 1) * slots]


def halo_sends(faces, tiles, d, grid, pw, pe, hw, he, north, south, corners, polar):
    s, t = lax.axis_index("face"), lax.axis_index("tile")
    rows, cols = grid.shape[0], grid.shape[1]
    east, west = lax.rem(s + 1, faces), lax.rem(s + faces - 1, faces)
    last, first = pl.ds(rows - d, d), pl.ds(0, d)
    right, left = pl.ds(cols - EDGE, EDGE), pl.ds(0, EDGE)
    not_top, not_low = t > 0, t < tiles - 1
    up, down = t - 1, t + 1
    plan = [
        (None, None, pe, hw, (east, t)),
        (None, None, pw, he, (west, t)),
        (not_low, not_top, grid.at[last], north, (s, down)),
        (not_top, not_low, grid.at[first], south, (s, up)),
        (not_low, not_top, grid.at[last, right], corners.at[0], (east, down)),
        (not_low, not_top, grid.at[last, left], corners.at[1], (west, down)),
        (not_top, not_low, grid.at[first, right], corners.at[2], (east, up)),
        (not_top, not_low, grid.at[first, left], corners.at[3], (west, up)),
    ]
    for k in range(1, faces):
        to = (lax.rem(s + k, faces), t)
        plan.append((t == 0, t == 0, grid.at[first], polar.at[s], to))
    for k in range(1, faces):
        to = (lax.rem(s + k, faces), t)
        plan.append((t == tiles - 1, t == tiles - 1, grid.at[last], polar.at[s], to))
    return plan


def guarded(cond, action):
    if cond is None:
        action()
    else:
        pl.when(cond)(action)


def start_halo(plan, send_sem, recv_sem):
    copies = []
    for i, (sends, receives, src, dst, to) in enumerate(plan):
        copy = pltpu.make_async_remote_copy(
            src_ref=src, dst_ref=dst, send_sem=send_sem.at[i], recv_sem=recv_sem.at[i],
            device_id=to, device_id_type=MESH,
        )
        guarded(sends, copy.start)
        copies.append((sends, receives, copy))
    return copies


def wait_received(copies):
    for _, receives, copy in copies:
        guarded(receives, copy.wait_recv)


def wait_sent(copies):
    for sends, _, copy in copies:
        guarded(sends, copy.wait_send)


def own_polar(grid, polar, d, tiles, sem):
    s, t = lax.axis_index("face"), lax.axis_index("tile")
    top = pltpu.make_async_copy(grid.at[pl.ds(0, d)], polar.at[s], sem)
    low = pltpu.make_async_copy(grid.at[pl.ds(grid.shape[0] - d, d)], polar.at[s], sem)
    return [(t == 0, top), (t == tiles - 1, low)]


def fill_columns(d, pad, rows, cols, hw, he):
    pad[d : d + rows, cols:] = jnp.concatenate(
        [unpack_columns(he[...], d, False), unpack_columns(hw[...], d, True)], axis=1
    ).astype(jnp.bfloat16)


def fill_ends(faces, tiles, d, pad, rows, cols, north, south, corners, polar, link, turn):
    s, t = lax.axis_index("face"), lax.axis_index("tile")
    wide = cols + EDGE

    def from_pole(base, column):
        p = link[column, s]
        east, west = lax.rem(p + 1, faces), lax.rem(p + faces - 1, faces)
        here = lax.broadcasted_iota(jnp.int32, (wide, wide), 0)
        there = lax.broadcasted_iota(jnp.int32, (wide, wide), 1)
        mirrored = jnp.where(here < cols, cols - 1 - here, wide + cols - 1 - here)
        source = jnp.where(turn[column, s] == 1, mirrored, here)
        move = jnp.where(there == source, 1.0, 0.0).astype(jnp.bfloat16)
        for i in range(d):
            k = d - 1 - i
            edge = join_edge(polar[east, k, :EDGE], polar[west, k, cols - EDGE :])
            line = jnp.concatenate([polar[p, k], edge], axis=0)
            pad[base + i] = jnp.dot(move, line, preferred_element_type=jnp.float32).astype(jnp.bfloat16)

    @pl.when(t == 0)
    def _():
        from_pole(0, 0)

    @pl.when(t > 0)
    def _():
        pad[:d, :cols] = north[...]
        pad[:d, cols:] = join_edge(corners[1], corners[0])

    @pl.when(t == tiles - 1)
    def _():
        from_pole(d + rows, 1)

    @pl.when(t < tiles - 1)
    def _():
        pad[d + rows :, :cols] = south[...]
        pad[d + rows :, cols:] = join_edge(corners[3], corners[2])


def fill_taps(taps, wide_taps):
    channels, features = taps.shape[1], taps.shape[2]
    for k in range(4):
        for e in range(3):
            for j in range(2):
                piece = (
                    taps[3 * (k - j) + e] if 0 <= k - j <= 2 else jnp.zeros((channels, features), jnp.bfloat16)
                )
                at = (2 * e + j) * features
                wide_taps[k * channels : (k + 1) * channels, at : at + features] = piece


def conv_rows(pad, wide_taps, bias, d, start, cols):
    wide = cols + EDGE
    features = bias.shape[-1]
    count = STEP // (2 * d)
    lines = []
    for k in range(4):
        blocks = [pad[pl.ds(start + m * 2 * d + k * d, d)] for m in range(count)]
        lines.append(jnp.concatenate(blocks, axis=0).reshape(count * d * wide, pad.shape[-1]))
    product = jnp.dot(
        jnp.concatenate(lines, axis=1), wide_taps[...], preferred_element_type=jnp.float32
    ).reshape(count * d, wide, 6 * features)
    halves = []
    for j in range(2):
        low, middle, high = (
            product[:, :, (2 * e + j) * features : (2 * e + j + 1) * features] for e in range(3)
        )
        total = pltpu.roll(low, d, 1) + middle + pltpu.roll(high, wide - d, 1)
        halves.append(total[:, :cols] + bias[...].reshape(1, 1, features))
    return [(m * 2 * d + j * d, halves[j][m * d : (m + 1) * d]) for m in range(count) for j in range(2)]


def fill_edge_taps(taps, edge_taps):
    channels, features = taps.shape[1], taps.shape[2]
    for a in range(3):
        for i, e in enumerate((0, 2)):
            edge_taps[a * channels : (a + 1) * channels, i * features : (i + 1) * features] = taps[3 * a + e]


def conv_inner(pad, wide_taps, bias, d, start, cols, edges):
    features = bias.shape[-1]
    count = STEP // (2 * d)
    lines = []
    for k in range(4):
        blocks = [pad[pl.ds(start + m * 2 * d + k * d, d), :cols] for m in range(count)]
        lines.append(jnp.concatenate(blocks, axis=0).reshape(count * d * cols, pad.shape[-1]))
    product = jnp.dot(
        jnp.concatenate(lines, axis=1), wide_taps[...], preferred_element_type=jnp.float32
    ).reshape(count * d, cols, 6 * features)
    shift = bias[...].reshape(1, 1, features)
    sub = lax.broadcasted_iota(jnp.int32, (count * d, 8, features), 1)
    pieces = []
    for j in range(2):
        low, middle, high = (
            product[:, :, (2 * e + j) * features : (2 * e + j + 1) * features] for e in range(3)
        )
        low = pltpu.roll(low, d, 1)
        high = pltpu.roll(high, cols - d, 1)
        middle = middle + shift
        left = middle[:, :8] + high[:, :8] + jnp.where(sub < d, 0.0, low[:, :8])
        right = middle[:, cols - 8 :] + low[:, cols - 8 :] + jnp.where(sub >= 8 - d, 0.0, high[:, cols - 8 :])
        total = low + middle + high
        for m in range(count):
            offset = m * 2 * d + j * d
            edges[0, pl.ds(start + offset, d)] = left[m * d : (m + 1) * d]
            edges[1, pl.ds(start + offset, d)] = right[m * d : (m + 1) * d]
            pieces.append((offset, total[m * d : (m + 1) * d]))
    return pieces


def finish_edges(pad, edge_taps, d, start, size, cols, edges, held, out):
    features = edges.shape[-1]
    lines = [
        pad[pl.ds(start + a * d, size), cols:].reshape(size * EDGE, pad.shape[-1]) for a in range(3)
    ]
    product = jnp.dot(
        jnp.concatenate(lines, axis=1), edge_taps[...], preferred_element_type=jnp.float32
    ).reshape(size, EDGE, 2 * features)
    sub = lax.broadcasted_iota(jnp.int32, (size, 8, features), 1)
    here = pl.ds(start, size)
    from_west = pltpu.roll(product[:, 8:, :features], d, 1)
    left = edges[0, here] + jnp.where(sub < d, from_west, 0.0)
    from_east = pltpu.roll(product[:, :8, features:], 8 - d, 1)
    right = edges[1, here] + jnp.where(sub >= 8 - d, from_east, 0.0)
    kept = out[here, :EDGE].astype(jnp.float32)[:, 8:]
    fresh = held[here, :EDGE].astype(jnp.float32)[:, :8] + jax.nn.gelu(left, approximate=True)
    out[here, :EDGE] = jnp.concatenate([fresh, kept], axis=1).astype(jnp.bfloat16)
    kept = out[here, cols - EDGE :].astype(jnp.float32)[:, :8]
    fresh = held[here, cols - EDGE :].astype(jnp.float32)[:, 8:] + jax.nn.gelu(right, approximate=True)
    out[here, cols - EDGE :] = jnp.concatenate([kept, fresh], axis=1).astype(jnp.bfloat16)


def first_kernel(
    faces, tiles, d, slots,
    link, turn, owner, cells, values, taps, bias, grid,
    first, rows_in, cells_in,
    pad, wide_taps, held, rows_out, cells_out, pw, pe, hw, he, north, south, corners, polar,
    send_sem, recv_sem, row_send, row_recv, cell_send, cell_recv, own_sem,
):
    rows, cols, channels = grid.shape
    cell_total = rows * cols
    count = faces * tiles
    me = lax.axis_index("face") * tiles + lax.axis_index("tile")
    barrier = pltpu.get_barrier_semaphore()
    load = pltpu.make_async_copy(grid, pad.at[pl.ds(d, rows), pl.ds(0, cols)], own_sem.at[3])
    load.start()

    def device(k):
        other = lax.rem(me + k, count)
        return other, (other // tiles, lax.rem(other, tiles))

    def greet(k, carry):
        _, to = device(k)
        pl.semaphore_signal(barrier, inc=1, device_id=to, device_id_type=MESH)
        return carry

    lax.fori_loop(1, count, greet, 0)
    own = own_polar(grid, polar, d, tiles, own_sem.at[2])
    for cond, copy in own:
        guarded(cond, copy.start)
    cells_out[...] = jnp.full(cells_out.shape, cell_total, jnp.int32)
    target, codes = rank_observations(count, slots, owner, cells)
    load.wait()
    pw[...] = pack_columns(pad[d : d + rows, :EDGE].astype(jnp.float32), d, False)
    pe[...] = pack_columns(pad[d : d + rows, cols - EDGE : cols].astype(jnp.float32), d, True)
    pl.semaphore_wait(barrier, count - 1)
    copies = start_halo(
        halo_sends(faces, tiles, d, grid, pw, pe, hw, he, north, south, corners, polar), send_sem, recv_sem
    )

    def row_copy(other):
        to = (other // tiles, lax.rem(other, tiles))
        return pltpu.make_async_remote_copy(
            src_ref=rows_out.at[other], dst_ref=rows_in.at[me],
            send_sem=row_send.at[lax.rem(other + count - me, count)],
            recv_sem=row_recv.at[lax.rem(other + count - me, count)],
            device_id=to, device_id_type=MESH,
        )

    def cell_copy(other):
        to = (other // tiles, lax.rem(other, tiles))
        return pltpu.make_async_remote_copy(
            src_ref=cells_out.at[other], dst_ref=cells_in.at[me],
            send_sem=cell_send.at[lax.rem(other + count - me, count)],
            recv_sem=cell_recv.at[lax.rem(other + count - me, count)],
            device_id=to, device_id_type=MESH,
        )

    def finish(k, carry):
        other = lax.rem(me + k, count)
        row_copy(other).wait()
        cell_copy(other).wait()
        return carry

    s, t = lax.axis_index("face"), lax.axis_index("tile")
    for b in range(1, faces + 1):
        face = lax.rem(s + b, faces)
        pack_block(tiles * slots, slots, cell_total, face, target, codes, values, rows_out, cells_out)

        def send(k, carry, face=face):
            other = face * tiles + lax.rem(t + k, tiles)
            row_copy(other).start()
            cell_copy(other).start()
            return carry

        lax.fori_loop(1 if b == faces else 0, tiles, send, 0)

    own_rows = pltpu.make_async_copy(rows_out.at[me], rows_in.at[me], own_sem.at[0])
    own_cells = pltpu.make_async_copy(cells_out.at[me], cells_in.at[me], own_sem.at[1])
    own_rows.start()
    own_cells.start()

    fill_taps(taps, wide_taps)
    wait_received(copies[:2])
    fill_columns(d, pad, rows, cols, hw, he)

    def step(i, carry):
        start = i * STEP
        for offset, piece in conv_rows(pad, wide_taps, bias, d, start, cols):
            at = pl.multiple_of((start + offset) * cols, d * cols)
            held[pl.ds(at, d * cols)] = jax.nn.gelu(piece, approximate=True).reshape(d * cols, channels)
        return carry

    steps = rows // STEP
    lax.fori_loop(1, steps - 1, step, 0, unroll=2)
    stores = []
    for i, (begin, size) in enumerate([(STEP, rows - 2 * STEP), (0, STEP), (rows - STEP, STEP)]):
        part = pl.ds(begin * cols, size * cols)
        stores.append(pltpu.make_async_copy(held.at[part], first.at[part], own_sem.at[4 + i]))
    stores[0].start()
    wait_received(copies[2:])
    for cond, copy in own:
        guarded(cond, copy.wait)
    fill_ends(faces, tiles, d, pad, rows, cols, north, south, corners, polar, link, turn)
    step(0, 0)
    step(steps - 1, 0)
    stores[1].start()
    stores[2].start()
    wait_sent(copies)
    own_rows.wait()
    own_cells.wait()
    lax.fori_loop(1, count, finish, 0)
    for store in stores:
        store.wait()


def inject_kernel(
    d_next, cells, first, values, weight, mixed_out, pw_out, pe_out,
    total, encoded, held, mixed, load_sem, store_sem,
):
    rows, cols, channels = mixed.shape
    sources, slots, features = values.shape
    cell_total = rows * cols
    size = rows // CHUNKS
    loads, stores = [], []
    for c in range(CHUNKS):
        part = pl.ds(c * size * cols, size * cols)
        loads.append(pltpu.make_async_copy(first.at[part], held.at[part], load_sem.at[c]))
        part = pl.ds(c * size, size)
        stores.append(pltpu.make_async_copy(mixed.at[part], mixed_out.at[part], store_sem.at[c]))
    for load in loads:
        load.start()
    encoded[...] = jnp.dot(
        values[...].reshape(sources * slots, features), weight[...], preferred_element_type=jnp.float32
    )
    total[...] = jnp.zeros_like(total)
    group = GROUP

    def add_group(i, carry):
        source, at = i // (slots // group), lax.rem(i, slots // group) * group
        marked = [cells[source, at + j] for j in range(group)]

        @pl.when(marked[0] < cell_total)
        def _():
            any_repeat = functools.reduce(lambda x, y: x | y, marked) & REPEAT
            places = [m & (REPEAT - 1) for m in marked]

            def row(j):
                return encoded[pl.ds(i * group + j, 1)]

            @pl.when(any_repeat == 0)
            def _():
                sums = [total[pl.ds(places[j], 1)] + row(j) for j in range(group)]
                for j in range(group):
                    total[pl.ds(places[j], 1)] = sums[j]

            @pl.when(any_repeat != 0)
            def _():
                for j in range(group):
                    total[pl.ds(places[j], 1)] += row(j)

        return carry

    lax.fori_loop(0, sources * slots // group, add_group, 0)

    def step(i, carry):
        at = pl.multiple_of(i * STEP * cols, STEP * cols)
        here = held[pl.ds(at, STEP * cols)] + total[pl.ds(at, STEP * cols)]
        mixed[pl.ds(i * STEP, STEP)] = here.astype(jnp.bfloat16).reshape(STEP, cols, channels)
        return carry

    for c in range(CHUNKS):
        loads[c].wait()
        lax.fori_loop(c * size // STEP, (c + 1) * size // STEP, step, 0)
        stores[c].start()
    pw_out[...] = pack_columns(mixed[:, :EDGE].astype(jnp.float32), d_next, False)
    pe_out[...] = pack_columns(mixed[:, cols - EDGE :].astype(jnp.float32), d_next, True)
    for store in stores:
        store.wait()


def second_kernel(
    faces, tiles, d, link, turn, taps, bias, grid, pw, pe, fields,
    out_ref,
    out, pad, wide_taps, held, edge_taps, edges, hw, he, north, south, corners, polar,
    send_sem, recv_sem, own_sem,
):
    rows, cols, channels = grid.shape
    s, t = lax.axis_index("face"), lax.axis_index("tile")
    barrier = pltpu.get_barrier_semaphore()

    def greet(to):
        pl.semaphore_signal(barrier, inc=1, device_id=to, device_id_type=MESH)

    east, west = lax.rem(s + 1, faces), lax.rem(s + faces - 1, faces)
    greet((east, t))
    greet((west, t))

    @pl.when(t > 0)
    def _():
        for f in (east, s, west):
            greet((f, t - 1))

    @pl.when(t < tiles - 1)
    def _():
        for f in (east, s, west):
            greet((f, t + 1))

    polar_end = (t == 0) | (t == tiles - 1)

    @pl.when(polar_end)
    def _():
        for k in range(2, faces - 1):
            greet((lax.rem(s + k, faces), t))

    own = own_polar(grid, polar, d, tiles, own_sem.at[0])
    for cond, copy in own:
        guarded(cond, copy.start)
    half = rows // 2
    loads = []
    for c in range(2):
        part = pl.ds(c * half, half)
        place = pad.at[pl.ds(d + c * half, half), pl.ds(0, cols)]
        loads.append((
            pltpu.make_async_copy(grid.at[part], place, own_sem.at[1 + c]),
            pltpu.make_async_copy(fields.at[part], held.at[part], own_sem.at[3 + c]),
        ))
    for pair in loads:
        for load in pair:
            load.start()

    @pl.when(polar_end)
    def _():
        pl.semaphore_wait(barrier, 5 + faces - 3)

    @pl.when(jnp.logical_not(polar_end))
    def _():
        pl.semaphore_wait(barrier, 8)

    copies = start_halo(
        halo_sends(faces, tiles, d, grid, pw, pe, hw, he, north, south, corners, polar), send_sem, recv_sem
    )
    fill_taps(taps, wide_taps)
    fill_edge_taps(taps, edge_taps)

    def write(start, pieces):
        for offset, piece in pieces:
            here = held[pl.ds(start + offset, d)].astype(jnp.float32)
            out[pl.ds(start + offset, d)] = (
                here + jax.nn.gelu(piece, approximate=True)
            ).astype(jnp.bfloat16)

    def inner(i, carry):
        write(i * STEP, conv_inner(pad, wide_taps, bias, d, i * STEP, cols, edges))
        return carry

    def finish(i, carry):
        finish_edges(pad, edge_taps, d, i * 2 * STEP + STEP, 2 * STEP, cols, edges, held, out)
        return carry

    steps = rows // STEP
    ready = (half - d) // STEP
    for pair, begin, end in ((loads[0], 1, ready), (loads[1], ready, steps - 1)):
        for load in pair:
            load.wait()
        lax.fori_loop(begin, end, inner, 0, unroll=2)
    wait_received(copies[:2])
    fill_columns(d, pad, rows, cols, hw, he)
    lax.fori_loop(0, (steps - 2) // 2, finish, 0)
    stores = []
    for i, (begin, size) in enumerate([(STEP, rows - 2 * STEP), (0, STEP), (rows - STEP, STEP)]):
        part = pl.ds(begin, size)
        stores.append(pltpu.make_async_copy(out.at[part], out_ref.at[part], own_sem.at[5 + i]))
    stores[0].start()
    wait_received(copies[2:])
    for cond, copy in own:
        guarded(cond, copy.wait)
    fill_ends(faces, tiles, d, pad, rows, cols, north, south, corners, polar, link, turn)
    for start in (0, rows - STEP):
        write(start, conv_rows(pad, wide_taps, bias, d, start, cols))
    stores[1].start()
    stores[2].start()
    wait_sent(copies)
    for store in stores:
        store.wait()


def local(
    fields, first_kernel_taps, first_conv_bias, second_kernel_taps, second_conv_bias,
    obs_weight, obs_values, obs_owner, obs_cells, polar_neighbor_sector, polar_link_reversal,
):
    faces, tiles = lax.axis_size("face"), lax.axis_size("tile")
    rows, cols, channels = fields.shape
    obs_rows, features = obs_values.shape
    dest_count = faces * tiles
    slots = 2 * obs_rows // dest_count
    cell_total = rows * cols
    bf16, f32, i32 = jnp.bfloat16, jnp.float32, jnp.int32
    shape = jax.ShapeDtypeStruct
    vmem = pl.BlockSpec(memory_space=pltpu.VMEM)
    smem = pl.BlockSpec(memory_space=pltpu.SMEM)
    anywhere = pl.BlockSpec(memory_space=pl.ANY)
    dma = pltpu.SemaphoreType.DMA
    d1, d2 = FIRST_DILATION, SECOND_DILATION
    halo_copies = 8 + 2 * (faces - 1)
    link, turn = polar_neighbor_sector.T, polar_link_reversal.T

    def packed_dims(d):
        return (rows * d // EDGE, EDGE, channels)

    def conv_scratch(d):
        return [
            pltpu.VMEM((rows + 2 * d, cols + EDGE, channels), bf16),
            pltpu.VMEM((4 * channels, 6 * channels), bf16),
        ]

    def halo_scratch(d):
        return [
            pltpu.VMEM(packed_dims(d), bf16), pltpu.VMEM(packed_dims(d), bf16),
            pltpu.VMEM((d, cols, channels), bf16), pltpu.VMEM((d, cols, channels), bf16),
            pltpu.VMEM((4, d, EDGE, channels), bf16), pltpu.VMEM((faces, d, cols, channels), bf16),
        ]

    first, recv_rows, recv_cells = pl.pallas_call(
        functools.partial(first_kernel, faces, tiles, d1, slots),
        out_shape=[
            shape((cell_total, channels), f32),
            shape((dest_count, slots, features), bf16),
            shape((dest_count, 1, LANES), i32),
        ],
        in_specs=[smem] * 2 + [vmem] * 5 + [anywhere],
        out_specs=[anywhere] * 3,
        scratch_shapes=conv_scratch(d1) + [
            pltpu.VMEM((cell_total, channels), f32),
            pltpu.VMEM((dest_count, slots, features), bf16),
            pltpu.VMEM((dest_count, 1, LANES), i32),
            pltpu.VMEM(packed_dims(d1), bf16), pltpu.VMEM(packed_dims(d1), bf16),
        ] + halo_scratch(d1) + [
            dma((halo_copies,)), dma((halo_copies,)), dma((dest_count,)), dma((dest_count,)),
            dma((dest_count,)), dma((dest_count,)), dma((7,)),
        ],
        compiler_params=pltpu.CompilerParams(
            collective_id=0, has_side_effects=True, vmem_limit_bytes=VMEM_LIMIT
        ),
        name="first_conv_and_exchange",
    )(
        link, turn, obs_owner.reshape(1, obs_rows), obs_cells.reshape(1, obs_rows), obs_values,
        first_kernel_taps, first_conv_bias.reshape(1, channels), fields,
    )

    mixed, pw, pe = pl.pallas_call(
        functools.partial(inject_kernel, d2),
        out_shape=[
            shape((rows, cols, channels), bf16), shape(packed_dims(d2), bf16), shape(packed_dims(d2), bf16)
        ],
        in_specs=[smem, anywhere, vmem, vmem],
        out_specs=[anywhere, vmem, vmem],
        scratch_shapes=[
            pltpu.VMEM((cell_total + 8, channels), f32),
            pltpu.VMEM((dest_count * slots, channels), f32),
            pltpu.VMEM((cell_total, channels), f32),
            pltpu.VMEM((rows, cols, channels), bf16),
            dma((CHUNKS,)), dma((CHUNKS,)),
        ],
        compiler_params=pltpu.CompilerParams(vmem_limit_bytes=VMEM_LIMIT),
        name="inject",
    )(recv_cells.reshape(dest_count, LANES), first, recv_rows, obs_weight)

    return pl.pallas_call(
        functools.partial(second_kernel, faces, tiles, d2),
        out_shape=shape((rows, cols, channels), bf16),
        in_specs=[smem] * 2 + [vmem] * 2 + [anywhere] * 4,
        out_specs=anywhere,
        scratch_shapes=[pltpu.VMEM((rows, cols, channels), bf16)] + conv_scratch(d2) + [
            pltpu.VMEM((rows, cols, channels), bf16),
            pltpu.VMEM((3 * channels, 2 * channels), bf16),
            pltpu.VMEM((2, rows, 8, channels), f32),
        ] + halo_scratch(d2) + [dma((halo_copies,)), dma((halo_copies,)), dma((8,))],
        compiler_params=pltpu.CompilerParams(
            collective_id=1, has_side_effects=True, vmem_limit_bytes=VMEM_LIMIT
        ),
        name="second_conv_and_exchange",
    )(
        link, turn, second_kernel_taps, second_conv_bias.reshape(1, channels), mixed, pw, pe, fields
    )


def solution(mesh):
    in_specs = (
        P("tile", "face", None), P(), P(), P(), P(), P(),
        P(("face", "tile"), None), P(("face", "tile"), None), P(("face", "tile")), P(), P(),
    )
    return jax.shard_map(
        local, mesh=mesh, in_specs=in_specs, out_specs=P("tile", "face", None), check_vma=False
    )
```

```python
import functools

import jax
import jax.numpy as jnp
from jax import lax
from jax.experimental import pallas as pl
from jax.experimental.pallas import tpu as pltpu
from jax.sharding import PartitionSpec as P

FIRST_DILATION = 2
SECOND_DILATION = 4
MESH = pl.DeviceIdType.MESH
LANES = 128
EDGE = 16
STEP = 8
GROUP = 16
REPEAT = 1 << 14
CHUNKS = 4
VMEM_LIMIT = 56 * 1024 * 1024


def pack_columns(tile, d, east):
    rows, _, ch = tile.shape
    per = 8 // d
    half = tile[:, 8:] if east else tile[:, :8]
    grouped = half.reshape(rows // per, per, 8, ch)
    sub = lax.broadcasted_iota(jnp.int32, (rows // per, 8, ch), 1)
    out = None
    for j in range(per):
        shift = (j * d - (8 - d if east else 0)) % 8
        part = grouped[:, j]
        if shift:
            part = pltpu.roll(part, shift, 1)
        out = part if out is None else jnp.where(sub >= j * d, part, out)
    return out.reshape(rows // (2 * per), EDGE, ch).astype(jnp.bfloat16)


def unpack_columns(packed, d, west):
    count, _, ch = packed.shape
    per = 8 // d
    pieces = packed.astype(jnp.float32).reshape(2 * count, 8, ch)
    parts = []
    for j in range(per):
        shift = ((8 - d if west else 0) - j * d) % 8
        parts.append(pltpu.roll(pieces, shift, 1) if shift else pieces)
    return jnp.stack(parts, axis=1).reshape(2 * count * per, 8, ch)


def join_edge(east_tile, west_tile):
    east = east_tile.astype(jnp.float32)
    west = west_tile.astype(jnp.float32)
    axis = east.ndim - 2
    return jnp.concatenate(
        [lax.slice_in_dim(east, 0, 8, axis=axis), lax.slice_in_dim(west, 8, 16, axis=axis)], axis=axis
    ).astype(jnp.bfloat16)


def rank_observations(dest_count, slots, owner_ref, cells_ref):
    obs = owner_ref.shape[1]
    owner = owner_ref[...]
    dests = lax.broadcasted_iota(jnp.int32, (dest_count, obs), 0)
    onehot = jnp.where(dests == owner, 1.0, 0.0)
    before = (
        lax.broadcasted_iota(jnp.int32, (obs, obs), 0) < lax.broadcasted_iota(jnp.int32, (obs, obs), 1)
    )
    ranks = jnp.dot(
        onehot.astype(jnp.bfloat16),
        jnp.where(before, 1.0, 0.0).astype(jnp.bfloat16),
        preferred_element_type=jnp.float32,
    )
    rank = jnp.sum(ranks * onehot, axis=0, keepdims=True).astype(jnp.int32)
    target = owner * slots + rank
    cells = cells_ref[...]
    kind = lax.broadcasted_iota(jnp.int32, (8, obs), 0)
    codes = jnp.where(kind == 0, cells >> 7, jnp.where(kind == 1, cells & 127, 1))
    codes = codes.astype(jnp.float32).astype(jnp.bfloat16)
    return target, codes


def pack_block(block, slots, cell_total, face, target, codes, values, rows_out, cells_out):
    obs = target.shape[1]
    first = face * (block // slots)
    wanted = face * block + lax.broadcasted_iota(jnp.int32, (block, obs), 0)
    match = jnp.where(wanted == target, 1.0, 0.0).astype(jnp.bfloat16)
    rows = jnp.dot(match, values[...], preferred_element_type=jnp.float32).astype(jnp.bfloat16)
    rows_out[pl.ds(first, block // slots)] = rows.reshape(block // slots, slots, rows.shape[-1])
    got = lax.dot_general(codes, match, (((1,), (1,)), ((), ())), preferred_element_type=jnp.float32)
    found = (got[0:1] * LANES + got[1:2]).astype(jnp.int32)
    found = jnp.broadcast_to(jnp.where(got[2:3] > 0.5, found, cell_total), (8, block))
    place = lax.broadcasted_iota(jnp.int32, (8, block), 1) & (GROUP - 1)
    repeats = jnp.zeros((8, block), jnp.int32)
    for k in range(1, GROUP):
        same = (found == pltpu.roll(found, k, 1)) & (place >= k) & (found < cell_total)
        repeats = jnp.where(same, REPEAT, repeats)
    found = found + repeats
    for j in range(block // slots):
        cells_out[first + j, :, :slots] = found[:1, j * slots : (j + 1) * slots]


def halo_sends(faces, tiles, d, grid, pw, pe, hw, he, north, south, corners, polar):
    s, t = lax.axis_index("face"), lax.axis_index("tile")
    rows, cols = grid.shape[0], grid.shape[1]
    east, west = lax.rem(s + 1, faces), lax.rem(s + faces - 1, faces)
    last, first = pl.ds(rows - d, d), pl.ds(0, d)
    right, left = pl.ds(cols - EDGE, EDGE), pl.ds(0, EDGE)
    not_top, not_low = t > 0, t < tiles - 1
    up, down = t - 1, t + 1
    plan = [
        (None, None, pe, hw, (east, t)),
        (None, None, pw, he, (west, t)),
        (not_low, not_top, grid.at[last], north, (s, down)),
        (not_top, not_low, grid.at[first], south, (s, up)),
        (not_low, not_top, grid.at[last, right], corners.at[0], (east, down)),
        (not_low, not_top, grid.at[last, left], corners.at[1], (west, down)),
        (not_top, not_low, grid.at[first, right], corners.at[2], (east, up)),
        (not_top, not_low, grid.at[first, left], corners.at[3], (west, up)),
    ]
    for k in range(1, faces):
        to = (lax.rem(s + k, faces), t)
        plan.append((t == 0, t == 0, grid.at[first], polar.at[s], to))
    for k in range(1, faces):
        to = (lax.rem(s + k, faces), t)
        plan.append((t == tiles - 1, t == tiles - 1, grid.at[last], polar.at[s], to))
    return plan


def guarded(cond, action):
    if cond is None:
        action()
    else:
        pl.when(cond)(action)


def start_halo(plan, send_sem, recv_sem):
    copies = []
    for i, (sends, receives, src, dst, to) in enumerate(plan):
        copy = pltpu.make_async_remote_copy(
            src_ref=src, dst_ref=dst, send_sem=send_sem.at[i], recv_sem=recv_sem.at[i],
            device_id=to, device_id_type=MESH,
        )
        guarded(sends, copy.start)
        copies.append((sends, receives, copy))
    return copies


def wait_received(copies):
    for _, receives, copy in copies:
        guarded(receives, copy.wait_recv)


def wait_sent(copies):
    for sends, _, copy in copies:
        guarded(sends, copy.wait_send)


def own_polar(grid, polar, d, tiles, sem):
    s, t = lax.axis_index("face"), lax.axis_index("tile")
    top = pltpu.make_async_copy(grid.at[pl.ds(0, d)], polar.at[s], sem)
    low = pltpu.make_async_copy(grid.at[pl.ds(grid.shape[0] - d, d)], polar.at[s], sem)
    return [(t == 0, top), (t == tiles - 1, low)]


def fill_columns(d, pad, rows, cols, hw, he):
    pad[d : d + rows, cols:] = jnp.concatenate(
        [unpack_columns(he[...], d, False), unpack_columns(hw[...], d, True)], axis=1
    ).astype(jnp.bfloat16)


def fill_ends(faces, tiles, d, pad, rows, cols, north, south, corners, polar, link, turn, which, then):
    s, t = lax.axis_index("face"), lax.axis_index("tile")
    wide = cols + EDGE

    def from_pole(base, column):
        p = link[column, s]
        east, west = lax.rem(p + 1, faces), lax.rem(p + faces - 1, faces)
        here = lax.broadcasted_iota(jnp.int32, (wide, wide), 0)
        there = lax.broadcasted_iota(jnp.int32, (wide, wide), 1)
        mirrored = jnp.where(here < cols, cols - 1 - here, wide + cols - 1 - here)
        source = jnp.where(turn[column, s] == 1, mirrored, here)
        move = jnp.where(there == source, 1.0, 0.0).astype(jnp.bfloat16)
        for i in range(d):
            k = d - 1 - i
            edge = join_edge(polar[east, k, :EDGE], polar[west, k, cols - EDGE :])
            line = jnp.concatenate([polar[p, k], edge], axis=0)
            pad[base + i] = jnp.dot(move, line, preferred_element_type=jnp.float32).astype(jnp.bfloat16)

    if which == "poles":

        @pl.when(t == 0)
        def _():
            from_pole(0, 0)
            then(0)

        @pl.when(t == tiles - 1)
        def _():
            from_pole(d + rows, 1)
            then(rows - STEP)

        return

    @pl.when(t > 0)
    def _():
        pad[:d, :cols] = north[...]
        pad[:d, cols:] = join_edge(corners[1], corners[0])
        then(0)

    @pl.when(t < tiles - 1)
    def _():
        pad[d + rows :, :cols] = south[...]
        pad[d + rows :, cols:] = join_edge(corners[3], corners[2])
        then(rows - STEP)


def fill_taps(taps, wide_taps):
    channels, features = taps.shape[1], taps.shape[2]
    for k in range(4):
        for e in range(3):
            for j in range(2):
                piece = (
                    taps[3 * (k - j) + e] if 0 <= k - j <= 2 else jnp.zeros((channels, features), jnp.bfloat16)
                )
                at = (2 * e + j) * features
                wide_taps[k * channels : (k + 1) * channels, at : at + features] = piece


def conv_rows(pad, wide_taps, bias, d, start, cols):
    wide = cols + EDGE
    features = bias.shape[-1]
    count = STEP // (2 * d)
    lines = []
    for k in range(4):
        blocks = [pad[pl.ds(start + m * 2 * d + k * d, d)] for m in range(count)]
        lines.append(jnp.concatenate(blocks, axis=0).reshape(count * d * wide, pad.shape[-1]))
    product = jnp.dot(
        jnp.concatenate(lines, axis=1), wide_taps[...], preferred_element_type=jnp.float32
    ).reshape(count * d, wide, 6 * features)
    halves = []
    for j in range(2):
        low, middle, high = (
            product[:, :, (2 * e + j) * features : (2 * e + j + 1) * features] for e in range(3)
        )
        total = pltpu.roll(low, d, 1) + middle + pltpu.roll(high, wide - d, 1)
        halves.append(total[:, :cols] + bias[...].reshape(1, 1, features))
    return [(m * 2 * d + j * d, halves[j][m * d : (m + 1) * d]) for m in range(count) for j in range(2)]


def fill_edge_taps(taps, edge_taps):
    channels, features = taps.shape[1], taps.shape[2]
    for a in range(3):
        for i, e in enumerate((0, 2)):
            edge_taps[a * channels : (a + 1) * channels, i * features : (i + 1) * features] = taps[3 * a + e]


def conv_inner(pad, wide_taps, bias, d, start, cols, edges):
    features = bias.shape[-1]
    count = STEP // (2 * d)
    lines = []
    for k in range(4):
        blocks = [pad[pl.ds(start + m * 2 * d + k * d, d), :cols] for m in range(count)]
        lines.append(jnp.concatenate(blocks, axis=0).reshape(count * d * cols, pad.shape[-1]))
    product = jnp.dot(
        jnp.concatenate(lines, axis=1), wide_taps[...], preferred_element_type=jnp.float32
    ).reshape(count * d, cols, 6 * features)
    shift = bias[...].reshape(1, 1, features)
    sub = lax.broadcasted_iota(jnp.int32, (count * d, 8, features), 1)
    pieces = []
    for j in range(2):
        low, middle, high = (
            product[:, :, (2 * e + j) * features : (2 * e + j + 1) * features] for e in range(3)
        )
        low = pltpu.roll(low, d, 1)
        high = pltpu.roll(high, cols - d, 1)
        middle = middle + shift
        left = middle[:, :8] + high[:, :8] + jnp.where(sub < d, 0.0, low[:, :8])
        right = middle[:, cols - 8 :] + low[:, cols - 8 :] + jnp.where(sub >= 8 - d, 0.0, high[:, cols - 8 :])
        total = low + middle + high
        for m in range(count):
            offset = m * 2 * d + j * d
            edges[0, pl.ds(start + offset, d)] = left[m * d : (m + 1) * d]
            edges[1, pl.ds(start + offset, d)] = right[m * d : (m + 1) * d]
            pieces.append((offset, total[m * d : (m + 1) * d]))
    return pieces


def finish_edges(pad, edge_taps, d, start, size, cols, edges, held, out):
    features = edges.shape[-1]
    lines = [
        pad[pl.ds(start + a * d, size), cols:].reshape(size * EDGE, pad.shape[-1]) for a in range(3)
    ]
    product = jnp.dot(
        jnp.concatenate(lines, axis=1), edge_taps[...], preferred_element_type=jnp.float32
    ).reshape(size, EDGE, 2 * features)
    sub = lax.broadcasted_iota(jnp.int32, (size, 8, features), 1)
    here = pl.ds(start, size)
    from_west = pltpu.roll(product[:, 8:, :features], d, 1)
    left = edges[0, here] + jnp.where(sub < d, from_west, 0.0)
    from_east = pltpu.roll(product[:, :8, features:], 8 - d, 1)
    right = edges[1, here] + jnp.where(sub >= 8 - d, from_east, 0.0)
    kept = out[here, :EDGE].astype(jnp.float32)[:, 8:]
    fresh = held[here, :EDGE].astype(jnp.float32)[:, :8] + jax.nn.gelu(left, approximate=True)
    out[here, :EDGE] = jnp.concatenate([fresh, kept], axis=1).astype(jnp.bfloat16)
    kept = out[here, cols - EDGE :].astype(jnp.float32)[:, :8]
    fresh = held[here, cols - EDGE :].astype(jnp.float32)[:, 8:] + jax.nn.gelu(right, approximate=True)
    out[here, cols - EDGE :] = jnp.concatenate([kept, fresh], axis=1).astype(jnp.bfloat16)


def first_kernel(
    faces, tiles, d, slots,
    link, turn, owner, cells, values, taps, bias, grid,
    first, rows_in, cells_in,
    pad, wide_taps, held, rows_out, cells_out, pw, pe, hw, he, north, south, corners, polar,
    send_sem, recv_sem, row_send, row_recv, cell_send, cell_recv, own_sem,
):
    rows, cols, channels = grid.shape
    cell_total = rows * cols
    count = faces * tiles
    me = lax.axis_index("face") * tiles + lax.axis_index("tile")
    barrier = pltpu.get_barrier_semaphore()
    load = pltpu.make_async_copy(grid, pad.at[pl.ds(d, rows), pl.ds(0, cols)], own_sem.at[3])
    load.start()

    def device(k):
        other = lax.rem(me + k, count)
        return other, (other // tiles, lax.rem(other, tiles))

    def greet(k, carry):
        _, to = device(k)
        pl.semaphore_signal(barrier, inc=1, device_id=to, device_id_type=MESH)
        return carry

    lax.fori_loop(1, count, greet, 0)
    own = own_polar(grid, polar, d, tiles, own_sem.at[2])
    for cond, copy in own:
        guarded(cond, copy.start)
    cells_out[...] = jnp.full(cells_out.shape, cell_total, jnp.int32)
    target, codes = rank_observations(count, slots, owner, cells)
    load.wait()
    pw[...] = pack_columns(pad[d : d + rows, :EDGE].astype(jnp.float32), d, False)
    pe[...] = pack_columns(pad[d : d + rows, cols - EDGE : cols].astype(jnp.float32), d, True)
    pl.semaphore_wait(barrier, count - 1)
    copies = start_halo(
        halo_sends(faces, tiles, d, grid, pw, pe, hw, he, north, south, corners, polar), send_sem, recv_sem
    )

    def row_copy(other):
        to = (other // tiles, lax.rem(other, tiles))
        return pltpu.make_async_remote_copy(
            src_ref=rows_out.at[other], dst_ref=rows_in.at[me],
            send_sem=row_send.at[lax.rem(other + count - me, count)],
            recv_sem=row_recv.at[lax.rem(other + count - me, count)],
            device_id=to, device_id_type=MESH,
        )

    def cell_copy(other):
        to = (other // tiles, lax.rem(other, tiles))
        return pltpu.make_async_remote_copy(
            src_ref=cells_out.at[other], dst_ref=cells_in.at[me],
            send_sem=cell_send.at[lax.rem(other + count - me, count)],
            recv_sem=cell_recv.at[lax.rem(other + count - me, count)],
            device_id=to, device_id_type=MESH,
        )

    def finish(k, carry):
        other = lax.rem(me + k, count)
        row_copy(other).wait()
        cell_copy(other).wait()
        return carry

    s, t = lax.axis_index("face"), lax.axis_index("tile")
    for b in range(1, faces + 1):
        face = lax.rem(s + b, faces)
        pack_block(tiles * slots, slots, cell_total, face, target, codes, values, rows_out, cells_out)

        def send(k, carry, face=face):
            other = face * tiles + lax.rem(t + k, tiles)
            row_copy(other).start()
            cell_copy(other).start()
            return carry

        lax.fori_loop(1 if b == faces else 0, tiles, send, 0)

    own_rows = pltpu.make_async_copy(rows_out.at[me], rows_in.at[me], own_sem.at[0])
    own_cells = pltpu.make_async_copy(cells_out.at[me], cells_in.at[me], own_sem.at[1])
    own_rows.start()
    own_cells.start()

    fill_taps(taps, wide_taps)
    wait_received(copies[:2])
    fill_columns(d, pad, rows, cols, hw, he)

    def step(i, carry):
        start = i * STEP
        for offset, piece in conv_rows(pad, wide_taps, bias, d, start, cols):
            at = pl.multiple_of((start + offset) * cols, d * cols)
            held[pl.ds(at, d * cols)] = jax.nn.gelu(piece, approximate=True).reshape(d * cols, channels)
        return carry

    steps = rows // STEP
    lax.fori_loop(1, steps - 1, step, 0, unroll=2)
    stores = []
    for i, (begin, size) in enumerate([(STEP, rows - 2 * STEP), (0, STEP), (rows - STEP, STEP)]):
        part = pl.ds(begin * cols, size * cols)
        stores.append(pltpu.make_async_copy(held.at[part], first.at[part], own_sem.at[4 + i]))
    stores[0].start()
    ends = (faces, tiles, d, pad, rows, cols, north, south, corners, polar, link, turn)
    wait_received(copies[2:8])
    fill_ends(*ends, "tiles", lambda start: step(start // STEP, 0))
    wait_received(copies[8:])
    for cond, copy in own:
        guarded(cond, copy.wait)
    fill_ends(*ends, "poles", lambda start: step(start // STEP, 0))
    stores[1].start()
    stores[2].start()
    wait_sent(copies)
    own_rows.wait()
    own_cells.wait()
    lax.fori_loop(1, count, finish, 0)
    for store in stores:
        store.wait()


def inject_kernel(
    d_next, cells, first, values, weight, mixed_out, pw_out, pe_out,
    total, encoded, held, mixed, load_sem, store_sem,
):
    rows, cols, channels = mixed.shape
    sources, slots, features = values.shape
    cell_total = rows * cols
    size = rows // CHUNKS
    loads, stores = [], []
    for c in range(CHUNKS):
        part = pl.ds(c * size * cols, size * cols)
        loads.append(pltpu.make_async_copy(first.at[part], held.at[part], load_sem.at[c]))
        part = pl.ds(c * size, size)
        stores.append(pltpu.make_async_copy(mixed.at[part], mixed_out.at[part], store_sem.at[c]))
    for load in loads:
        load.start()
    encoded[...] = jnp.dot(
        values[...].reshape(sources * slots, features), weight[...], preferred_element_type=jnp.float32
    )
    total[...] = jnp.zeros_like(total)
    group = GROUP

    def add_group(i, carry):
        source, at = i // (slots // group), lax.rem(i, slots // group) * group
        marked = [cells[source, at + j] for j in range(group)]

        @pl.when(marked[0] < cell_total)
        def _():
            any_repeat = functools.reduce(lambda x, y: x | y, marked) & REPEAT
            places = [m & (REPEAT - 1) for m in marked]

            def row(j):
                return encoded[pl.ds(i * group + j, 1)]

            @pl.when(any_repeat == 0)
            def _():
                sums = [total[pl.ds(places[j], 1)] + row(j) for j in range(group)]
                for j in range(group):
                    total[pl.ds(places[j], 1)] = sums[j]

            @pl.when(any_repeat != 0)
            def _():
                for j in range(group):
                    total[pl.ds(places[j], 1)] += row(j)

        return carry

    lax.fori_loop(0, sources * slots // group, add_group, 0)

    def step(i, carry):
        at = pl.multiple_of(i * STEP * cols, STEP * cols)
        here = held[pl.ds(at, STEP * cols)] + total[pl.ds(at, STEP * cols)]
        mixed[pl.ds(i * STEP, STEP)] = here.astype(jnp.bfloat16).reshape(STEP, cols, channels)
        return carry

    for c in range(CHUNKS):
        loads[c].wait()
        lax.fori_loop(c * size // STEP, (c + 1) * size // STEP, step, 0)
        stores[c].start()
    pw_out[...] = pack_columns(mixed[:, :EDGE].astype(jnp.float32), d_next, False)
    pe_out[...] = pack_columns(mixed[:, cols - EDGE :].astype(jnp.float32), d_next, True)
    for store in stores:
        store.wait()


def second_kernel(
    faces, tiles, d, link, turn, taps, bias, grid, pw, pe, fields,
    out_ref,
    out, pad, wide_taps, held, edge_taps, edges, hw, he, north, south, corners, polar,
    send_sem, recv_sem, own_sem,
):
    rows, cols, channels = grid.shape
    s, t = lax.axis_index("face"), lax.axis_index("tile")
    barrier = pltpu.get_barrier_semaphore()

    def greet(to):
        pl.semaphore_signal(barrier, inc=1, device_id=to, device_id_type=MESH)

    east, west = lax.rem(s + 1, faces), lax.rem(s + faces - 1, faces)
    greet((east, t))
    greet((west, t))

    @pl.when(t > 0)
    def _():
        for f in (east, s, west):
            greet((f, t - 1))

    @pl.when(t < tiles - 1)
    def _():
        for f in (east, s, west):
            greet((f, t + 1))

    polar_end = (t == 0) | (t == tiles - 1)

    @pl.when(polar_end)
    def _():
        for k in range(2, faces - 1):
            greet((lax.rem(s + k, faces), t))

    own = own_polar(grid, polar, d, tiles, own_sem.at[0])
    for cond, copy in own:
        guarded(cond, copy.start)
    half = rows // 2
    loads = []
    for c in range(2):
        part = pl.ds(c * half, half)
        place = pad.at[pl.ds(d + c * half, half), pl.ds(0, cols)]
        loads.append((
            pltpu.make_async_copy(grid.at[part], place, own_sem.at[1 + c]),
            pltpu.make_async_copy(fields.at[part], held.at[part], own_sem.at[3 + c]),
        ))
    for pair in loads:
        for load in pair:
            load.start()

    @pl.when(polar_end)
    def _():
        pl.semaphore_wait(barrier, 5 + faces - 3)

    @pl.when(jnp.logical_not(polar_end))
    def _():
        pl.semaphore_wait(barrier, 8)

    copies = start_halo(
        halo_sends(faces, tiles, d, grid, pw, pe, hw, he, north, south, corners, polar), send_sem, recv_sem
    )
    fill_taps(taps, wide_taps)
    fill_edge_taps(taps, edge_taps)

    def write(start, pieces):
        for offset, piece in pieces:
            here = held[pl.ds(start + offset, d)].astype(jnp.float32)
            out[pl.ds(start + offset, d)] = (
                here + jax.nn.gelu(piece, approximate=True)
            ).astype(jnp.bfloat16)

    def inner(i, carry):
        write(i * STEP, conv_inner(pad, wide_taps, bias, d, i * STEP, cols, edges))
        return carry

    def finish(i, carry):
        finish_edges(pad, edge_taps, d, i * 2 * STEP + STEP, 2 * STEP, cols, edges, held, out)
        return carry

    steps = rows // STEP
    ready = (half - d) // STEP
    for pair, begin, end in ((loads[0], 1, ready), (loads[1], ready, steps - 1)):
        for load in pair:
            load.wait()
        lax.fori_loop(begin, end, inner, 0, unroll=2)
    wait_received(copies[:2])
    fill_columns(d, pad, rows, cols, hw, he)
    lax.fori_loop(0, (steps - 2) // 2, finish, 0)
    stores = []
    for i, (begin, size) in enumerate([(STEP, rows - 2 * STEP), (0, STEP), (rows - STEP, STEP)]):
        part = pl.ds(begin, size)
        stores.append(pltpu.make_async_copy(out.at[part], out_ref.at[part], own_sem.at[5 + i]))
    stores[0].start()

    def finish_end(start):
        write(start, conv_rows(pad, wide_taps, bias, d, start, cols))

    ends = (faces, tiles, d, pad, rows, cols, north, south, corners, polar, link, turn)
    wait_received(copies[2:8])
    fill_ends(*ends, "tiles", finish_end)
    wait_received(copies[8:])
    for cond, copy in own:
        guarded(cond, copy.wait)
    fill_ends(*ends, "poles", finish_end)
    stores[1].start()
    stores[2].start()
    wait_sent(copies)
    for store in stores:
        store.wait()


def local(
    fields, first_kernel_taps, first_conv_bias, second_kernel_taps, second_conv_bias,
    obs_weight, obs_values, obs_owner, obs_cells, polar_neighbor_sector, polar_link_reversal,
):
    faces, tiles = lax.axis_size("face"), lax.axis_size("tile")
    rows, cols, channels = fields.shape
    obs_rows, features = obs_values.shape
    dest_count = faces * tiles
    slots = 2 * obs_rows // dest_count
    cell_total = rows * cols
    bf16, f32, i32 = jnp.bfloat16, jnp.float32, jnp.int32
    shape = jax.ShapeDtypeStruct
    vmem = pl.BlockSpec(memory_space=pltpu.VMEM)
    smem = pl.BlockSpec(memory_space=pltpu.SMEM)
    anywhere = pl.BlockSpec(memory_space=pl.ANY)
    dma = pltpu.SemaphoreType.DMA
    d1, d2 = FIRST_DILATION, SECOND_DILATION
    halo_copies = 8 + 2 * (faces - 1)
    link, turn = polar_neighbor_sector.T, polar_link_reversal.T

    def packed_dims(d):
        return (rows * d // EDGE, EDGE, channels)

    def conv_scratch(d):
        return [
            pltpu.VMEM((rows + 2 * d, cols + EDGE, channels), bf16),
            pltpu.VMEM((4 * channels, 6 * channels), bf16),
        ]

    def halo_scratch(d):
        return [
            pltpu.VMEM(packed_dims(d), bf16), pltpu.VMEM(packed_dims(d), bf16),
            pltpu.VMEM((d, cols, channels), bf16), pltpu.VMEM((d, cols, channels), bf16),
            pltpu.VMEM((4, d, EDGE, channels), bf16), pltpu.VMEM((faces, d, cols, channels), bf16),
        ]

    first, recv_rows, recv_cells = pl.pallas_call(
        functools.partial(first_kernel, faces, tiles, d1, slots),
        out_shape=[
            shape((cell_total, channels), f32),
            shape((dest_count, slots, features), bf16),
            shape((dest_count, 1, LANES), i32),
        ],
        in_specs=[smem] * 2 + [vmem] * 5 + [anywhere],
        out_specs=[anywhere] * 3,
        scratch_shapes=conv_scratch(d1) + [
            pltpu.VMEM((cell_total, channels), f32),
            pltpu.VMEM((dest_count, slots, features), bf16),
            pltpu.VMEM((dest_count, 1, LANES), i32),
            pltpu.VMEM(packed_dims(d1), bf16), pltpu.VMEM(packed_dims(d1), bf16),
        ] + halo_scratch(d1) + [
            dma((halo_copies,)), dma((halo_copies,)), dma((dest_count,)), dma((dest_count,)),
            dma((dest_count,)), dma((dest_count,)), dma((7,)),
        ],
        compiler_params=pltpu.CompilerParams(
            collective_id=0, has_side_effects=True, vmem_limit_bytes=VMEM_LIMIT
        ),
        name="first_conv_and_exchange",
    )(
        link, turn, obs_owner.reshape(1, obs_rows), obs_cells.reshape(1, obs_rows), obs_values,
        first_kernel_taps, first_conv_bias.reshape(1, channels), fields,
    )

    mixed, pw, pe = pl.pallas_call(
        functools.partial(inject_kernel, d2),
        out_shape=[
            shape((rows, cols, channels), bf16), shape(packed_dims(d2), bf16), shape(packed_dims(d2), bf16)
        ],
        in_specs=[smem, anywhere, vmem, vmem],
        out_specs=[anywhere, vmem, vmem],
        scratch_shapes=[
            pltpu.VMEM((cell_total + 8, channels), f32),
            pltpu.VMEM((dest_count * slots, channels), f32),
            pltpu.VMEM((cell_total, channels), f32),
            pltpu.VMEM((rows, cols, channels), bf16),
            dma((CHUNKS,)), dma((CHUNKS,)),
        ],
        compiler_params=pltpu.CompilerParams(vmem_limit_bytes=VMEM_LIMIT),
        name="inject",
    )(recv_cells.reshape(dest_count, LANES), first, recv_rows, obs_weight)

    return pl.pallas_call(
        functools.partial(second_kernel, faces, tiles, d2),
        out_shape=shape((rows, cols, channels), bf16),
        in_specs=[smem] * 2 + [vmem] * 2 + [anywhere] * 4,
        out_specs=anywhere,
        scratch_shapes=[pltpu.VMEM((rows, cols, channels), bf16)] + conv_scratch(d2) + [
            pltpu.VMEM((rows, cols, channels), bf16),
            pltpu.VMEM((3 * channels, 2 * channels), bf16),
            pltpu.VMEM((2, rows, 8, channels), f32),
        ] + halo_scratch(d2) + [dma((halo_copies,)), dma((halo_copies,)), dma((8,))],
        compiler_params=pltpu.CompilerParams(
            collective_id=1, has_side_effects=True, vmem_limit_bytes=VMEM_LIMIT
        ),
        name="second_conv_and_exchange",
    )(
        link, turn, second_kernel_taps, second_conv_bias.reshape(1, channels), mixed, pw, pe, fields
    )


def solution(mesh):
    in_specs = (
        P("tile", "face", None), P(), P(), P(), P(), P(),
        P(("face", "tile"), None), P(("face", "tile"), None), P(("face", "tile")), P(), P(),
    )
    return jax.shard_map(
        local, mesh=mesh, in_specs=in_specs, out_specs=P("tile", "face", None), check_vma=False
    )
```
